32 devices in a mesh: row: 8 (over z, x), col: 4 (over y, core).
Axes of the slice: x: 2, y: 2, z: 4, core: 2. Of those that a mesh axis runs over, the one named last changes fastest.
Arguments:
- density: bfloat16 [4096, 1536], P(('row', 'col')), may hold values from -0.625 to 0.625
- pattern: int32 [32, 12], P(('row', 'col')), may hold values from 0 to 1, as said below
Outputs:
- band: bfloat16 [4096, 8, 512], P('row', None, 'col')
The draws below stay inside these ranges and needn't reach their ends.
Inputs may be any that keep to these rules, and one draw needn't show every extreme that they name: `pattern`: each block row has its own share of stored blocks.
All inputs are finite; a program needn't handle non-finite values.
Results may differ from the reference program's by a relative error of at most 0.001.
Values may be sent and summed in bfloat16 or wider, within the bound.
A program may use at most 64 MiB of HBM per device.

```python
import jax
import jax.numpy as jnp

BLOCK = 128
KB = 12
ROWS = 4096
STEPS = 8
N_ROW = 8
N_COL = 4


def draw_pattern(key, part):
    first_key, second_key = jax.random.split(jax.random.fold_in(key, 17))
    level = jax.random.randint(first_key, (ROWS // BLOCK, 1), 1, 9)
    ticket = jax.random.randint(second_key, (ROWS // BLOCK, KB), 0, 8)
    return (ticket < level).astype(jnp.int32)


def levels(stream_key, dims, pieces, smallest, top_value):
    def one(dim, shards_of):
        steps = jax.random.uniform(jax.random.fold_in(jax.random.fold_in(stream_key, 6), dim), (shards_of,), jnp.float32, smallest / len(pieces), top_value / len(pieces))
        return jnp.repeat(jnp.exp(steps), dims[dim] // shards_of).reshape((-1,) + (1,) * (len(dims) - dim - 1))

    loudness = one(*pieces[0])
    for cut in pieces[1:]:
        loudness = loudness * one(*cut)
    return loudness


def centred(key, dims, deviation, most, shards=(), kind=jnp.bfloat16):
    factor_of = levels(key, dims, shards, -0.22, 0.18) if shards else 1.0
    result = jax.random.normal(key, dims, jnp.float32) * deviation * factor_of
    return jnp.minimum(jnp.maximum(result, -most), most).astype(kind)


def setup_inputs(seed: int = 0) -> dict:
    key_of = jax.random.split(jax.random.key(seed), 3)
    return {
        "density": centred(key_of[0], (ROWS, KB * BLOCK), (KB * BLOCK // 16) ** -0.5, 0.625, ((0, 32),)),
        "pattern": draw_pattern(jax.random.fold_in(key_of[2], 71), 0),
    }


def reference(density, pattern):
    repeated = jnp.repeat(pattern, BLOCK, axis=0).astype(jnp.bfloat16)
    masked = (density.reshape(ROWS, KB, BLOCK) * repeated[:, :, None]).reshape(ROWS, KB * BLOCK)
    groups = masked.reshape(N_ROW, N_COL * BLOCK, KB * BLOCK).astype(jnp.float32)
    results = []
    for turn in range(STEPS):
        partner = jnp.roll(groups, -(N_ROW // 4 - turn), axis=0)
        product = jnp.einsum("rik,rjk->rij", groups, partner)
        results.append(product.astype(jnp.bfloat16).reshape(ROWS, N_COL * BLOCK))
    return jnp.stack(results, axis=1)
```

```python
import functools

import jax
import jax.numpy as jnp
from jax import lax
from jax.experimental import pallas as pl
from jax.experimental.pallas import tpu as pltpu
from jax.sharding import PartitionSpec as P

MESH = pl.DeviceIdType.MESH
CHUNKS = 2


def kernel(
    rows_n, cols_n, dens, pat, out, rowb, gb, ob, pb,
    r_row, r_gb, r_ob, s_up, s_dn, s_dup, s_x, s_y, s_c, s_p, s_out,
):
    zn, yn = rows_n // 2, cols_n // 2
    length, width = dens.shape
    group = cols_n * length
    part = length // CHUNKS
    half_span = rows_n // 4
    g, c = lax.axis_index("row"), lax.axis_index("col")
    z, x = g // 2, lax.rem(g, 2)
    y, k = c // 2, lax.rem(c, 2)
    low, high = z == 0, z == zn - 1
    edge = low | high
    inner = jnp.logical_not(edge)
    proxy = (z == 1) | (z == zn - 2)
    away = jnp.where((z == 1) | low, 1, jnp.where((z == zn - 2) | high, -1, 1))
    inward = z + away
    ze = z - away

    def row_of(zz, xx):
        return zz * 2 + xx

    def when(cond, action):
        pl.when(cond)(action)

    def dev_z(zz):
        return (row_of(zz, x), c)

    dev_x = (row_of(z, 1 - x), c)
    dev_k = (g, y * 2 + 1 - k)

    def dev_y(d):
        return (g, lax.rem(y + d, yn) * 2 + k)

    barrier = pltpu.get_barrier_semaphore()

    def greet(device):
        pl.semaphore_signal(barrier, inc=1, device_id=device, device_id_type=MESH)

    greet(dev_x)
    greet(dev_k)
    for d in range(1, yn):
        greet(dev_y(d))
    when(z > 0, lambda: greet(dev_z(z - 1)))
    when(z < zn - 1, lambda: greet(dev_z(z + 1)))

    def rows_at(n):
        return pl.ds(n * part, part)

    def gb_rows(cc, n):
        return pl.ds(pl.multiple_of(cc * length + n * part, part), part)

    blocks = pat.shape[0]
    size = length // blocks
    c0 = pl.multiple_of(c * length, length)
    for b in range(blocks):
        for kb in range(pat.shape[1]):
            here = dens[b * size:(b + 1) * size, kb * size:(kb + 1) * size]
            keep = jnp.broadcast_to(pat[b:b + 1, kb:kb + 1], here.shape) != 0
            kept = jnp.where(keep, here.astype(jnp.float32), 0.0).astype(here.dtype)
            rowb[z, x, b * size:(b + 1) * size, kb * size:(kb + 1) * size] = kept
            gb[0, pl.ds(c0 + b * size, size), kb * size:(kb + 1) * size] = kept

    def remote(src, dst, send, recv, device):
        return pltpu.make_async_remote_copy(
            src_ref=src, dst_ref=dst, send_sem=send, recv_sem=recv,
            device_id=device, device_id_type=MESH,
        )

    def row_copy(zz, xx, n, send, device):
        ref = rowb.at[zz, xx, rows_at(n)]
        return remote(ref, ref, send, r_row.at[zz, xx, n], device)

    def up(zz, n):
        return row_copy(zz, x, n, s_up.at[zz, n], dev_z(z + 1))

    def down(zz, n):
        return row_copy(zz, x, n, s_dn.at[zz, n], dev_z(z - 1))

    def double(n):
        return row_copy(z, 1 - x, n, s_dup.at[n], dev_z(inward))

    def across(zz, n):
        return row_copy(zz, x, n, s_x.at[zz, n], dev_x)

    def gb_send(p, src, cc, n, send, device):
        return remote(src, gb.at[p, gb_rows(cc, n)], send, r_gb.at[p, cc, n], device)

    def sideways(p, d, n):
        src = gb.at[0, gb_rows(c, n)] if p == 0 else rowb.at[ze, x, rows_at(n)]
        return gb_send(p, src, c, n, s_y.at[p, d, n], dev_y(d))

    def to_twin(p, d, n):
        cc = lax.rem(y + d, yn) * 2 + k
        if p == 1 and d == 0:
            src = rowb.at[ze, x, rows_at(n)]
        else:
            src = gb.at[p, gb_rows(cc, n)]
        return gb_send(p, src, cc, n, s_c.at[p, d, n], dev_k)

    def got_row(zz, xx, n):
        row_copy(zz, xx, n, s_dup.at[n], dev_x).wait_recv()

    def got_gb(p, cc, n):
        ref = gb.at[p, gb_rows(cc, n)]
        remote(ref, ref, s_dup.at[n], r_gb.at[p, cc, n], dev_x).wait_recv()

    def own_sends(n, do):
        for d in range(1, yn):
            do(sideways(0, d, n))
        do(across(z, n))
        when(z < zn - 1, lambda: do(up(z, n)))
        when(z > 0, lambda: do(down(z, n)))
        do(to_twin(0, 0, n))

    def y_arrivals(p, n, do, wait):
        for d in range(1, yn):
            if wait:
                got_gb(p, lax.rem(y + d, yn) * 2 + k, n)
            do(to_twin(p, d, n))

    def relay(zz, n, do):
        @pl.when((zz < z) & (z + 1 <= zn - 2))
        def _():
            do(up(zz, n))

        @pl.when((zz > z) & (z - 1 >= 1))
        def _():
            do(down(zz, n))

        adjacent = proxy & (zz == ze)

        @pl.when(jnp.logical_not(adjacent))
        def _():
            do(across(zz, n))

        @pl.when(adjacent)
        def _():
            for d in range(1, yn):
                do(sideways(1, d, n))
            do(to_twin(1, 0, n))

    def inside(zz):
        return (zz >= 0) & (zz <= zn - 1)

    def start(copy):
        copy.start()

    def finish(copy):
        copy.wait_send()

    step_rows = min(group, 512)

    def product(p, zz, xx, target, slot):
        def body(i, carry):
            at = pl.ds(pl.multiple_of(i * step_rows, step_rows), step_rows)
            target[slot, at, :] = lax.dot_general(
                gb[p, at, :], rowb[zz, xx], (((1,), (1,)), ((), ())),
                preferred_element_type=jnp.float32,
            ).astype(target.dtype)
            return carry

        if group == step_rows:
            body(0, 0)
        else:
            lax.fori_loop(0, group // step_rows, body, 0)

    def slot_of(gg, q):
        return lax.rem(gg + half_span - q + rows_n, rows_n)

    def out_copy(s):
        return pltpu.make_async_copy(ob.at[s], out.at[s], s_out.at[s])

    def own_job(zz, xx):
        s = slot_of(g, row_of(zz, xx))
        product(0, zz, xx, ob, s)
        out_copy(s).start()

    def proxy_copy(q):
        s = slot_of(row_of(ze, x), q)
        return remote(pb.at[q], ob.at[s], s_p.at[q], r_ob.at[s], dev_z(ze))

    def proxy_job(zz, xx):
        q = row_of(zz, xx)
        product(1, zz, xx, pb, q)
        proxy_copy(q).start()

    def all_twin(p):
        for n in range(CHUNKS):
            for d in range(yn):
                got_gb(p, lax.rem(y + d, yn) * 2 + 1 - k, n)

    neighbours = 2 + (yn - 1)
    pl.semaphore_wait(barrier, neighbours + jnp.where(edge, 1, 2))

    for n in range(CHUNKS):
        own_sends(n, start)

    @pl.when(edge)
    def _():
        for n in range(CHUNKS):
            y_arrivals(0, n, start, True)
            got_row(z, 1 - x, n)
            double(n).start()
            got_row(inward, x, n)
            across(inward, n).start()
        all_twin(0)

        def job(j, carry):
            zz = jnp.where(j < 2, z, inward)
            xx = jnp.where(lax.rem(j, 2) == 0, x, 1 - x)

            @pl.when(j == 3)
            def _():
                for n in range(CHUNKS):
                    got_row(inward, 1 - x, n)

            own_job(zz, xx)
            return carry

        lax.fori_loop(0, 4, job, 0)

        def far(i, carry):
            zz = inward + away * (i // 2 + 1)
            xx = jnp.where(lax.rem(i, 2) == 0, x, 1 - x)
            s = slot_of(g, row_of(zz, xx))
            remote(ob.at[s], ob.at[s], s_p.at[0], r_ob.at[s], dev_x).wait_recv()
            out_copy(s).start()
            return carry

        lax.fori_loop(0, 2 * (zn - 2), far, 0)

    @pl.when(inner)
    def _():
        def turn(t, carry):
            for n in range(CHUNKS):
                @pl.when(t == 1)
                def _():
                    y_arrivals(0, n, start, True)

                @pl.when((t == 2) & proxy)
                def _():
                    y_arrivals(1, n, start, True)

                for zz in (z - t * away, z + t * away):
                    @pl.when(inside(zz))
                    def _():
                        got_row(zz, x, n)
                        relay(zz, n, start)

            @pl.when(t == 1)
            def _():
                all_twin(0)

            @pl.when((t == 2) & proxy)
            def _():
                gb[1, pl.ds(c0, length), :] = rowb[ze, x]
                all_twin(1)

            def job(j, inner_carry):
                dist = jnp.where(j < 3, t - 1, t)
                sign = jnp.where((j == 2) | (j == 4), -away, away)
                zz = z + sign * dist
                other = (j == 1) | (j == 2)
                xx = jnp.where(other, 1 - x, x)
                valid = inside(zz) & jnp.where(
                    j == 0, t <= 2, jnp.where(j == 2, t >= 2, True)
                )

                @pl.when(valid & other)
                def _():
                    for n in range(CHUNKS):
                        got_row(zz, 1 - x, n)

                @pl.when(
                    valid & proxy & (t >= 2) & ((j == 0) | (j == 1) | (j == 3))
                )
                def _():
                    proxy_job(zz, xx)

                @pl.when(valid & jnp.where(j == 0, t == 1, True))
                def _():
                    own_job(zz, xx)

                return inner_carry

            lax.fori_loop(0, 5, job, 0)
            return carry

        lax.fori_loop(1, zn, turn, 0)

    for n in range(CHUNKS):
        own_sends(n, finish)
        y_arrivals(0, n, finish, False)

    @pl.when(edge)
    def _():
        for n in range(CHUNKS):
            double(n).wait_send()
            across(inward, n).wait_send()

    @pl.when(inner)
    def _():
        @pl.when(proxy)
        def _():
            for n in range(CHUNKS):
                y_arrivals(1, n, finish, False)

            def sent(i, carry):
                zz = z + away * (i // 2 + 1)
                proxy_copy(row_of(zz, lax.rem(i, 2))).wait_send()
                return carry

            lax.fori_loop(0, 2 * (zn - 2), sent, 0)

        def relayed(zz, carry):
            @pl.when(zz != z)
            def _():
                for n in range(CHUNKS):
                    relay(zz, n, finish)

            return carry

        lax.fori_loop(0, zn, relayed, 0)

    def stored(s, carry):
        out_copy(s).wait()
        return carry

    lax.fori_loop(0, rows_n, stored, 0)


def local(density, pattern):
    rows_n, cols_n = lax.axis_size("row"), lax.axis_size("col")
    length, width = density.shape
    group = cols_n * length
    zn, yn = rows_n // 2, cols_n // 2
    kind = density.dtype
    dma = pltpu.SemaphoreType.DMA
    words = (2 * rows_n * group * length + (2 * group + rows_n * length + 2 * length) * width)
    out = pl.pallas_call(
        functools.partial(kernel, rows_n, cols_n),
        out_shape=jax.ShapeDtypeStruct((rows_n, group, length), kind),
        in_specs=[pl.BlockSpec(memory_space=pltpu.VMEM)] * 2,
        out_specs=pl.BlockSpec(memory_space=pl.ANY),
        scratch_shapes=[
            pltpu.VMEM((zn, 2, length, width), kind),
            pltpu.VMEM((2, group, width), kind),
            pltpu.VMEM((rows_n, group, length), kind),
            pltpu.VMEM((rows_n, group, length), kind),
            dma((zn, 2, CHUNKS)),
            dma((2, cols_n, CHUNKS)),
            dma((rows_n,)),
            dma((zn, CHUNKS)),
            dma((zn, CHUNKS)),
            dma((CHUNKS,)),
            dma((zn, CHUNKS)),
            dma((2, yn, CHUNKS)),
            dma((2, yn, CHUNKS)),
            dma((rows_n,)),
            dma((rows_n,)),
        ],
        compiler_params=pltpu.CompilerParams(
            collective_id=0, has_side_effects=True, vmem_limit_bytes=2 * words + (8 << 20)
        ),
        cost_estimate=pl.CostEstimate(
            flops=2 * group * length * width * rows_n,
            bytes_accessed=2 * rows_n * group * length,
            transcendentals=0,
        ),
    )(density, pattern)
    return jnp.transpose(out, (1, 0, 2))


def solution(mesh):
    return jax.shard_map(
        local,
        mesh=mesh,
        in_specs=(P(("row", "col"), None), P(("row", "col"), None)),
        out_specs=P("row", None, "col"),
        check_vma=False,
    )
```

```python
import functools

import jax
import jax.numpy as jnp
from jax import lax
from jax.experimental import pallas as pl
from jax.experimental.pallas import tpu as pltpu
from jax.sharding import PartitionSpec as P

MESH = pl.DeviceIdType.MESH
CHUNKS = 4
HALF = CHUNKS // 2


def kernel(
    rows_n, cols_n, dens_hbm, pat_hbm, out, dens, pat, rowb, gb, ob, pb, s_in,
    r_row, r_gb, r_ob, s_up, s_dn, s_dup, s_x, s_y, s_c, s_p, s_out,
):
    fetch_dens = pltpu.make_async_copy(dens_hbm, dens, s_in.at[0])
    fetch_pat = pltpu.make_async_copy(pat_hbm, pat, s_in.at[1])
    fetch_dens.start()
    fetch_pat.start()
    zn, yn = rows_n // 2, cols_n // 2
    length, width = dens.shape
    group = cols_n * length
    part = length // CHUNKS
    half_span = rows_n // 4
    g, c = lax.axis_index("row"), lax.axis_index("col")
    z, x = g // 2, lax.rem(g, 2)
    y, k = c // 2, lax.rem(c, 2)
    low, high = z == 0, z == zn - 1
    edge = low | high
    inner = jnp.logical_not(edge)
    proxy = (z == 1) | (z == zn - 2)
    away = jnp.where((z == 1) | low, 1, jnp.where((z == zn - 2) | high, -1, 1))
    inward = z + away
    ze = z - away

    def row_of(zz, xx):
        return zz * 2 + xx

    def when(cond, action):
        pl.when(cond)(action)

    def dev_z(zz):
        return (row_of(zz, x), c)

    dev_x = (row_of(z, 1 - x), c)
    dev_k = (g, y * 2 + 1 - k)

    def dev_y(d):
        return (g, lax.rem(y + d, yn) * 2 + k)

    barrier = pltpu.get_barrier_semaphore()

    def greet(device):
        pl.semaphore_signal(barrier, inc=1, device_id=device, device_id_type=MESH)

    greet(dev_x)
    greet(dev_k)
    for d in range(1, yn):
        greet(dev_y(d))
    when(z > 0, lambda: greet(dev_z(z - 1)))
    when(z < zn - 1, lambda: greet(dev_z(z + 1)))

    def rows_at(xx, n):
        return pl.ds(pl.multiple_of(xx * length + n * part, part), part)

    def gb_rows(cc, n):
        return pl.ds(pl.multiple_of(cc * length + n * part, part), part)

    blocks = pat.shape[0]
    size = length // blocks
    c0 = pl.multiple_of(c * length, length)
    x0 = pl.multiple_of(x * length, length)
    fetch_dens.wait()
    fetch_pat.wait()
    for b in range(blocks):
        for kb in range(pat.shape[1]):
            here = dens[b * size:(b + 1) * size, kb * size:(kb + 1) * size]
            keep = jnp.broadcast_to(pat[b:b + 1, kb:kb + 1], here.shape) != 0
            kept = jnp.where(keep, here.astype(jnp.float32), 0.0).astype(here.dtype)
            rowb[z, pl.ds(x0 + b * size, size), kb * size:(kb + 1) * size] = kept
            gb[0, pl.ds(c0 + b * size, size), kb * size:(kb + 1) * size] = kept

    def remote(src, dst, send, recv, device):
        return pltpu.make_async_remote_copy(
            src_ref=src, dst_ref=dst, send_sem=send, recv_sem=recv,
            device_id=device, device_id_type=MESH,
        )

    def row_copy(zz, xx, n, send, device):
        ref = rowb.at[zz, rows_at(xx, n)]
        return remote(ref, ref, send, r_row.at[zz, xx, n], device)

    def up(zz, n):
        return row_copy(zz, x, n, s_up.at[zz, n], dev_z(z + 1))

    def down(zz, n):
        return row_copy(zz, x, n, s_dn.at[zz, n], dev_z(z - 1))

    def double(zz, n):
        return row_copy(zz, 1 - x, n, s_dup.at[n], dev_z(inward))

    def across(zz, n):
        return row_copy(zz, x, n, s_x.at[zz, n], dev_x)

    def gb_send(p, src, cc, n, send, device):
        return remote(src, gb.at[p, gb_rows(cc, n)], send, r_gb.at[p, cc, n], device)

    def sideways(p, d, n):
        src = gb.at[0, gb_rows(c, n)] if p == 0 else rowb.at[ze, rows_at(x, n)]
        return gb_send(p, src, c, n, s_y.at[p, d, n], dev_y(d))

    def to_twin(p, d, n):
        cc = lax.rem(y + d, yn) * 2 + k
        if p == 1 and d == 0:
            src = rowb.at[ze, rows_at(x, n)]
        else:
            src = gb.at[p, gb_rows(cc, n)]
        return gb_send(p, src, cc, n, s_c.at[p, d, n], dev_k)

    def got_row(zz, xx, n):
        row_copy(zz, xx, n, s_dup.at[n], dev_x).wait_recv()

    def got_gb(p, cc, n):
        ref = gb.at[p, gb_rows(cc, n)]
        remote(ref, ref, s_dup.at[n], r_gb.at[p, cc, n], dev_x).wait_recv()

    def own_sideways(n, do):
        for d in range(1, yn):
            do(sideways(0, d, n))

    def own_sends(n, do):
        do(across(z, n))
        when(z < zn - 1, lambda: do(up(z, n)))
        when(z > 0, lambda: do(down(z, n)))
        do(to_twin(0, 0, n))

    def y_arrivals(p, n, do, wait):
        for d in range(1, yn):
            if wait:
                got_gb(p, lax.rem(y + d, yn) * 2 + k, n)
            do(to_twin(p, d, n))

    def relay(zz, n, do):
        @pl.when((zz < z) & (z + 1 <= zn - 2))
        def _():
            do(up(zz, n))

        @pl.when((zz > z) & (z - 1 >= 1))
        def _():
            do(down(zz, n))

        dist = jnp.abs(zz - z)
        twice = ((zz == 0) | (zz == zn - 1)) & (
            (dist == 1) | ((dist == 2) & (n >= HALF))
        )

        @pl.when(jnp.logical_not(twice))
        def _():
            do(across(zz, n))

        adjacent = proxy & (zz == ze)

        @pl.when(adjacent)
        def _():
            for d in range(1, yn):
                do(sideways(1, d, n))
            do(to_twin(1, 0, n))

    def inside(zz):
        return (zz >= 0) & (zz <= zn - 1)

    def start(copy):
        copy.start()

    def finish(copy):
        copy.wait_send()

    step_rows = min(group, 256)

    def product(p, panel, store):
        def body(i, carry):
            at = pl.ds(pl.multiple_of(i * step_rows, step_rows), step_rows)
            store(at, lax.dot_general(
                gb[p, at, :], panel[...], (((1,), (1,)), ((), ())),
                preferred_element_type=jnp.float32,
            ).astype(ob.dtype))
            return carry

        lax.fori_loop(0, group // step_rows, body, 0)

    def slot_of(gg, q):
        return lax.rem(gg + half_span - q + rows_n, rows_n)

    def out_copy(s):
        return pltpu.make_async_copy(ob.at[s], out.at[s], s_out.at[s])

    def own_job(zz):
        slots = [slot_of(g, row_of(zz, xx)) for xx in range(2)]

        def store(at, value):
            for xx in range(2):
                ob[slots[xx], at, :] = value[:, xx * length:(xx + 1) * length]

        product(0, rowb.at[zz], store)
        for xx in range(2):
            out_copy(slots[xx]).start()

    def proxy_copy(q):
        s = slot_of(row_of(ze, x), q)
        return remote(pb.at[q], ob.at[s], s_p.at[q], r_ob.at[s], dev_z(ze))

    def proxy_job(zz, xx):
        q = row_of(zz, xx)

        def store(at, value):
            pb[q, at, :] = value

        product(1, rowb.at[zz, pl.ds(pl.multiple_of(xx * length, length), length)], store)
        proxy_copy(q).start()

    def all_twin(p):
        for n in range(CHUNKS):
            for d in range(yn):
                got_gb(p, lax.rem(y + d, yn) * 2 + 1 - k, n)

    neighbours = 2 + (yn - 1)
    pl.semaphore_wait(barrier, neighbours + jnp.where(edge, 1, 2))

    for n in range(CHUNKS):
        own_sends(n, start)

        @pl.when(edge | (n < HALF))
        def _():
            own_sideways(n, start)

    @pl.when(edge)
    def _():
        for n in range(CHUNKS):
            y_arrivals(0, n, start, True)
            got_row(z, 1 - x, n)
            double(z, n).start()
            got_row(inward, x, n)
            across(inward, n).start()
        all_twin(0)

        def job(j, carry):
            @pl.when(j == 1)
            def _():
                for n in range(CHUNKS):
                    got_row(inward, 1 - x, n)

            own_job(jnp.where(j == 0, z, inward))
            return carry

        lax.fori_loop(0, 2, job, 0)

        def far(i, carry):
            zz = inward + away * (i // 2 + 1)
            xx = jnp.where(lax.rem(i, 2) == 0, x, 1 - x)
            s = slot_of(g, row_of(zz, xx))
            remote(ob.at[s], ob.at[s], s_p.at[0], r_ob.at[s], dev_x).wait_recv()
            out_copy(s).start()
            return carry

        lax.fori_loop(0, 2 * (zn - 2), far, 0)

    @pl.when(inner)
    def _():
        def turn(t, carry):
            first, second = t == 1, t == 2

            def forwards(n):
                for zz in (z - t * away, z + t * away):
                    @pl.when(inside(zz))
                    def _():
                        got_row(zz, x, n)
                        relay(zz, n, start)

                @pl.when(second & proxy)
                def _():
                    got_row(ze, 1 - x, n)
                    if n >= HALF:
                        double(ze, n).start()

            def sides(early, late):
                @pl.when(first)
                def _():
                    for n in early:
                        y_arrivals(0, n, start, True)

                @pl.when(second)
                def _():
                    for n in late:
                        y_arrivals(0, n, start, True)

            def proxied(dist, xx):
                @pl.when(proxy & (dist >= 1) & inside(z + dist * away))
                def _():
                    proxy_job(z + dist * away, xx)

            for n in range(HALF):
                forwards(n)
                sides([n], [])

            @pl.when(second & proxy)
            def _():
                for n in range(CHUNKS):
                    y_arrivals(1, n, start, True)
                all_twin(1)
                proxied(t - 1, x)

            for n in range(HALF, CHUNKS):
                forwards(n)
                sides([], [n])

            @pl.when(first)
            def _():
                for n in range(HALF, CHUNKS):
                    own_sideways(n, start)

            @pl.when(first & proxy)
            def _():
                gb[1, pl.ds(c0, length), :] = rowb[ze, pl.ds(x0, length), :]

            @pl.when(second)
            def _():
                for n in range(CHUNKS):
                    got_row(z, 1 - x, n)

            def job(j, inner_carry):
                dist = jnp.where(j == 0, t - 1, t)
                xx = jnp.where(j == 0, 1 - x, x)

                @pl.when(j == 0)
                def _():
                    for zz in (z - (t - 1) * away, z + (t - 1) * away):
                        @pl.when(inside(zz) & jnp.logical_not(proxy & (zz == ze)))
                        def _():
                            for n in range(CHUNKS):
                                got_row(zz, 1 - x, n)

                proxied(dist, xx)
                return inner_carry

            @pl.when(t > 1)
            def _():
                lax.fori_loop(0, 2, job, 0)

            @pl.when(second)
            def _():
                all_twin(0)

            def own(j, inner_carry):
                dist = jnp.where(j == 0, 0, t - 1)
                zz = z + jnp.where(j == 1, -dist, dist) * away

                @pl.when(inside(zz) & ((j > 0) | second))
                def _():
                    own_job(zz)

                return inner_carry

            @pl.when(t > 1)
            def _():
                lax.fori_loop(0, 3, own, 0)

            return carry

        lax.fori_loop(1, zn, turn, 0)

    for n in range(CHUNKS):
        own_sends(n, finish)
        own_sideways(n, finish)
        y_arrivals(0, n, finish, False)

    @pl.when(edge)
    def _():
        for n in range(CHUNKS):
            double(z, n).wait_send()
            across(inward, n).wait_send()

    @pl.when(inner)
    def _():
        @pl.when(proxy)
        def _():
            for n in range(CHUNKS):
                y_arrivals(1, n, finish, False)
            for n in range(HALF, CHUNKS):
                double(ze, n).wait_send()

            def sent(i, carry):
                zz = z + away * (i // 2 + 1)
                proxy_copy(row_of(zz, lax.rem(i, 2))).wait_send()
                return carry

            lax.fori_loop(0, 2 * (zn - 2), sent, 0)

        def relayed(zz, carry):
            @pl.when(zz != z)
            def _():
                for n in range(CHUNKS):
                    relay(zz, n, finish)

            return carry

        lax.fori_loop(0, zn, relayed, 0)

    def stored(s, carry):
        out_copy(s).wait()
        return carry

    lax.fori_loop(0, rows_n, stored, 0)


def local(density, pattern):
    rows_n, cols_n = lax.axis_size("row"), lax.axis_size("col")
    length, width = density.shape
    group = cols_n * length
    zn, yn = rows_n // 2, cols_n // 2
    kind = density.dtype
    dma = pltpu.SemaphoreType.DMA
    words = (2 * rows_n * group * length + (2 * group + rows_n * length + 2 * length) * width)
    out = pl.pallas_call(
        functools.partial(kernel, rows_n, cols_n),
        out_shape=jax.ShapeDtypeStruct((rows_n, group, length), kind),
        in_specs=[pl.BlockSpec(memory_space=pltpu.HBM)] * 2,
        out_specs=pl.BlockSpec(memory_space=pl.ANY),
        scratch_shapes=[
            pltpu.VMEM((length, width), kind),
            pltpu.VMEM(pattern.shape, pattern.dtype),
            pltpu.VMEM((zn, 2 * length, width), kind),
            pltpu.VMEM((2, group, width), kind),
            pltpu.VMEM((rows_n, group, length), kind),
            pltpu.VMEM((rows_n, group, length), kind),
            dma((2,)),
            dma((zn, 2, CHUNKS)),
            dma((2, cols_n, CHUNKS)),
            dma((rows_n,)),
            dma((zn, CHUNKS)),
            dma((zn, CHUNKS)),
            dma((CHUNKS,)),
            dma((zn, CHUNKS)),
            dma((2, yn, CHUNKS)),
            dma((2, yn, CHUNKS)),
            dma((rows_n,)),
            dma((rows_n,)),
        ],
        compiler_params=pltpu.CompilerParams(
            collective_id=0, has_side_effects=True, vmem_limit_bytes=max(2 * words + (8 << 20), 56 << 20)
        ),
        cost_estimate=pl.CostEstimate(
            flops=2 * group * length * width * rows_n,
            bytes_accessed=2 * rows_n * group * length,
            transcendentals=0,
        ),
    )(density, pattern)
    return jnp.transpose(out, (1, 0, 2))


def solution(mesh):
    return jax.shard_map(
        local,
        mesh=mesh,
        in_specs=(P(("row", "col"), None), P(("row", "col"), None)),
        out_specs=P("row", None, "col"),
        check_vma=False,
    )
```

```python
import functools

import jax
import jax.numpy as jnp
from jax import lax
from jax.experimental import pallas as pl
from jax.experimental.pallas import tpu as pltpu
from jax.sharding import PartitionSpec as P

MESH = pl.DeviceIdType.MESH
CHUNKS = 4
HALF = CHUNKS // 2
LAST = CHUNKS - 1


def kernel(
    rows_n, cols_n, dens_hbm, pat_hbm, ob, dens, pat, rowb, gb, pb, s_in,
    r_row, r_gb, r_ob, s_up, s_dn, s_dup, s_x, s_y, s_c, s_p,
):
    fetch_dens = pltpu.make_async_copy(dens_hbm, dens, s_in.at[0])
    fetch_pat = pltpu.make_async_copy(pat_hbm, pat, s_in.at[1])
    fetch_dens.start()
    fetch_pat.start()
    zn, yn = rows_n // 2, cols_n // 2
    length, width = dens.shape
    group = cols_n * length
    part = length // CHUNKS
    half_span = rows_n // 4
    g, c = lax.axis_index("row"), lax.axis_index("col")
    z, x = g // 2, lax.rem(g, 2)
    y, k = c // 2, lax.rem(c, 2)
    low, high = z == 0, z == zn - 1
    edge = low | high
    inner = jnp.logical_not(edge)
    proxy = (z == 1) | (z == zn - 2)
    away = jnp.where((z == 1) | low, 1, jnp.where((z == zn - 2) | high, -1, 1))
    inward = z + away
    ze = z - away

    def row_of(zz, xx):
        return zz * 2 + xx

    def when(cond, action):
        pl.when(cond)(action)

    def dev_z(zz):
        return (row_of(zz, x), c)

    dev_x = (row_of(z, 1 - x), c)
    dev_k = (g, y * 2 + 1 - k)

    def dev_y(d):
        return (g, lax.rem(y + d, yn) * 2 + k)

    barrier = pltpu.get_barrier_semaphore()

    def greet(device):
        pl.semaphore_signal(barrier, inc=1, device_id=device, device_id_type=MESH)

    greet(dev_x)
    greet(dev_k)
    for d in range(1, yn):
        greet(dev_y(d))
    when(z > 0, lambda: greet(dev_z(z - 1)))
    when(z < zn - 1, lambda: greet(dev_z(z + 1)))

    def rows_at(xx, n):
        return pl.ds(pl.multiple_of(xx * length + n * part, part), part)

    def gb_rows(cc, n):
        return pl.ds(pl.multiple_of(cc * length + n * part, part), part)

    blocks = pat.shape[0]
    size = length // blocks
    c0 = pl.multiple_of(c * length, length)
    x0 = pl.multiple_of(x * length, length)
    fetch_dens.wait()
    fetch_pat.wait()
    for b in range(blocks):
        for kb in range(pat.shape[1]):
            here = dens[b * size:(b + 1) * size, kb * size:(kb + 1) * size]
            keep = jnp.broadcast_to(pat[b:b + 1, kb:kb + 1], here.shape) != 0
            kept = jnp.where(keep, here.astype(jnp.float32), 0.0).astype(here.dtype)
            rowb[z, pl.ds(x0 + b * size, size), kb * size:(kb + 1) * size] = kept
            gb[0, pl.ds(c0 + b * size, size), kb * size:(kb + 1) * size] = kept

    def remote(src, dst, send, recv, device):
        return pltpu.make_async_remote_copy(
            src_ref=src, dst_ref=dst, send_sem=send, recv_sem=recv,
            device_id=device, device_id_type=MESH,
        )

    def row_copy(zz, xx, n, send, device):
        ref = rowb.at[zz, rows_at(xx, n)]
        return remote(ref, ref, send, r_row.at[zz, xx, n], device)

    def up(zz, n):
        return row_copy(zz, x, n, s_up.at[zz, n], dev_z(z + 1))

    def down(zz, n):
        return row_copy(zz, x, n, s_dn.at[zz, n], dev_z(z - 1))

    def double(zz, n):
        return row_copy(zz, 1 - x, n, s_dup.at[jnp.where(zz == z, 0, 1), n], dev_z(inward))

    def across(zz, n):
        return row_copy(zz, x, n, s_x.at[zz, n], dev_x)

    def gb_send(p, src, cc, n, send, device):
        return remote(src, gb.at[p, gb_rows(cc, n)], send, r_gb.at[p, cc, n], device)

    def sideways(p, d, n):
        src = gb.at[0, gb_rows(c, n)] if p == 0 else rowb.at[ze, rows_at(x, n)]
        return gb_send(p, src, c, n, s_y.at[p, d, n], dev_y(d))

    def to_twin(p, d, n):
        cc = lax.rem(y + d, yn) * 2 + k
        if p == 1 and d == 0:
            src = rowb.at[ze, rows_at(x, n)]
        else:
            src = gb.at[p, gb_rows(cc, n)]
        return gb_send(p, src, cc, n, s_c.at[p, d, n], dev_k)

    def got_row(zz, xx, n):
        row_copy(zz, xx, n, s_dup.at[0, n], dev_x).wait_recv()

    def got_gb(p, cc, n):
        ref = gb.at[p, gb_rows(cc, n)]
        remote(ref, ref, s_dup.at[0, n], r_gb.at[p, cc, n], dev_x).wait_recv()

    def own_sideways(n, do):
        for d in range(1, yn):
            do(sideways(0, d, n))

    def own_sends(n, do):
        if n < HALF:
            do(across(z, n))
        else:
            when(jnp.logical_not(proxy), lambda: do(across(z, n)))
        when(z < zn - 1, lambda: do(up(z, n)))
        when(z > 0, lambda: do(down(z, n)))
        do(to_twin(0, 0, n))

    def y_arrivals(p, n, do, wait):
        for d in range(1, yn):
            if wait:
                got_gb(p, lax.rem(y + d, yn) * 2 + k, n)
            do(to_twin(p, d, n))

    def relay(zz, n, do):
        @pl.when((zz < z) & (z + 1 <= zn - 2))
        def _():
            do(up(zz, n))

        @pl.when((zz > z) & (z - 1 >= 1))
        def _():
            do(down(zz, n))

        dist = jnp.abs(zz - z)
        twice = ((zz == 0) | (zz == zn - 1)) & (
            (dist == 1) | ((dist == 2) & (n >= LAST))
        )

        @pl.when(jnp.logical_not(twice))
        def _():
            do(across(zz, n))

        adjacent = proxy & (zz == ze)

        @pl.when(adjacent)
        def _():
            for d in range(1, yn):
                do(sideways(1, d, n))
            do(to_twin(1, 0, n))

    def inside(zz):
        return (zz >= 0) & (zz <= zn - 1)

    def start(copy):
        copy.start()

    def finish(copy):
        copy.wait_send()

    step_rows = min(group, 256)

    def product(p, panel, store):
        def body(i, carry):
            at = pl.ds(pl.multiple_of(i * step_rows, step_rows), step_rows)
            store(at, lax.dot_general(
                gb[p, at, :], panel[...], (((1,), (1,)), ((), ())),
                preferred_element_type=jnp.float32,
            ).astype(ob.dtype))
            return carry

        lax.fori_loop(0, group // step_rows, body, 0)

    def slot_of(gg, q):
        return lax.rem(gg + half_span - q + rows_n, rows_n)

    def own_job(zz):
        slots = [slot_of(g, row_of(zz, xx)) for xx in range(2)]

        def store(at, value):
            for xx in range(2):
                ob[slots[xx], at, :] = value[:, xx * length:(xx + 1) * length]

        product(0, rowb.at[zz], store)

    def proxy_copy(q):
        s = slot_of(row_of(ze, x), q)
        return remote(pb.at[q], ob.at[s], s_p.at[q], r_ob.at[s], dev_z(ze))

    def proxy_job(zz, xx):
        q = row_of(zz, xx)

        def store(at, value):
            pb[q, at, :] = value

        product(1, rowb.at[zz, pl.ds(pl.multiple_of(xx * length, length), length)], store)
        proxy_copy(q).start()

    def all_twin(p):
        for n in range(CHUNKS):
            for d in range(yn):
                got_gb(p, lax.rem(y + d, yn) * 2 + 1 - k, n)

    neighbours = 2 + (yn - 1)
    pl.semaphore_wait(barrier, neighbours + jnp.where(edge, 1, 2))

    for n in range(CHUNKS):
        own_sends(n, start)

        @pl.when(edge | (n < HALF))
        def _():
            own_sideways(n, start)

    @pl.when(edge)
    def _():
        for n in range(CHUNKS):
            y_arrivals(0, n, start, True)
            got_row(z, 1 - x, n)
            double(z, n).start()
            got_row(inward, x, n)
            across(inward, n).start()
        all_twin(0)

        def job(j, carry):
            @pl.when(j == 1)
            def _():
                for n in range(CHUNKS):
                    got_row(inward, 1 - x, n)
                    if n >= HALF:
                        double(inward, n).start()

            own_job(jnp.where(j == 0, z, inward))
            return carry

        lax.fori_loop(0, 2, job, 0)

        def far(i, carry):
            zz = inward + away * (i // 2 + 1)
            xx = jnp.where(lax.rem(i, 2) == 0, x, 1 - x)
            s = slot_of(g, row_of(zz, xx))
            remote(ob.at[s], ob.at[s], s_p.at[0], r_ob.at[s], dev_x).wait_recv()
            return carry

        lax.fori_loop(0, 2 * (zn - 2), far, 0)

    @pl.when(inner)
    def _():
        def turn(t, carry):
            first, second = t == 1, t == 2

            def forwards(n):
                for zz in (z - t * away, z + t * away):
                    @pl.when(inside(zz))
                    def _():
                        got_row(zz, x, n)
                        relay(zz, n, start)

                @pl.when(second & proxy)
                def _():
                    got_row(ze, 1 - x, n)
                    if n >= LAST:
                        double(ze, n).start()

            def sides(early, late):
                @pl.when(first)
                def _():
                    for n in early:
                        y_arrivals(0, n, start, True)

                @pl.when(second)
                def _():
                    for n in late:
                        y_arrivals(0, n, start, True)

            def proxied(dist, xx):
                @pl.when(proxy & (dist >= 1) & inside(z + dist * away))
                def _():
                    proxy_job(z + dist * away, xx)

            def got_other(zz):
                @pl.when(inside(zz) & jnp.logical_not(proxy & (zz == ze)))
                def _():
                    for n in range(CHUNKS):
                        got_row(zz, 1 - x, n)

            for n in range(HALF):
                forwards(n)
                sides([n], [])

            @pl.when(second & proxy)
            def _():
                for n in range(CHUNKS):
                    y_arrivals(1, n, start, True)
                all_twin(1)
                proxied(t - 1, x)

            for n in range(HALF, CHUNKS):
                if n == LAST:
                    @pl.when(t > 1)
                    def _():
                        got_other(z + (t - 1) * away)
                        proxied(t - 1, 1 - x)
                forwards(n)
                sides([], [n])

            @pl.when(first)
            def _():
                for n in range(HALF, CHUNKS):
                    own_sideways(n, start)

            @pl.when(first & proxy)
            def _():
                gb[1, pl.ds(c0, length), :] = rowb[ze, pl.ds(x0, length), :]

            @pl.when(t > 1)
            def _():
                proxied(t, x)
                got_other(z - (t - 1) * away)

            @pl.when(second)
            def _():
                all_twin(0)

            def own(j, inner_carry):
                zz = z + jnp.where(j == 0, 1 - t, jnp.where(j == 1, t - 1, 0)) * away
                last = j == 2

                @pl.when(last & (t == zn - 1))
                def _():
                    for n in range(CHUNKS):
                        got_row(z, 1 - x, n)

                @pl.when(inside(zz) & (jnp.logical_not(last) | (t == zn - 1)))
                def _():
                    own_job(zz)

                return inner_carry

            @pl.when(t > 1)
            def _():
                lax.fori_loop(0, 3, own, 0)

            return carry

        lax.fori_loop(1, zn, turn, 0)

    for n in range(CHUNKS):
        own_sends(n, finish)
        own_sideways(n, finish)
        y_arrivals(0, n, finish, False)

    @pl.when(edge)
    def _():
        for n in range(CHUNKS):
            double(z, n).wait_send()
            across(inward, n).wait_send()
            if n >= HALF:
                double(inward, n).wait_send()

    @pl.when(inner)
    def _():
        @pl.when(proxy)
        def _():
            for n in range(CHUNKS):
                y_arrivals(1, n, finish, False)
            for n in range(LAST, CHUNKS):
                double(ze, n).wait_send()

            def sent(i, carry):
                zz = z + away * (i // 2 + 1)
                proxy_copy(row_of(zz, lax.rem(i, 2))).wait_send()
                return carry

            lax.fori_loop(0, 2 * (zn - 2), sent, 0)

        def relayed(zz, carry):
            @pl.when(zz != z)
            def _():
                for n in range(CHUNKS):
                    relay(zz, n, finish)

            return carry

        lax.fori_loop(0, zn, relayed, 0)


def local(density, pattern):
    rows_n, cols_n = lax.axis_size("row"), lax.axis_size("col")
    length, width = density.shape
    group = cols_n * length
    zn, yn = rows_n // 2, cols_n // 2
    kind = density.dtype
    dma = pltpu.SemaphoreType.DMA
    words = (2 * rows_n * group * length + (2 * group + rows_n * length + 2 * length) * width)
    out = pl.pallas_call(
        functools.partial(kernel, rows_n, cols_n),
        out_shape=jax.ShapeDtypeStruct((rows_n, group, length), kind),
        in_specs=[pl.BlockSpec(memory_space=pltpu.HBM)] * 2,
        out_specs=pl.BlockSpec(memory_space=pltpu.VMEM),
        scratch_shapes=[
            pltpu.VMEM((length, width), kind),
            pltpu.VMEM(pattern.shape, pattern.dtype),
            pltpu.VMEM((zn, 2 * length, width), kind),
            pltpu.VMEM((2, group, width), kind),
            pltpu.VMEM((rows_n, group, length), kind),
            dma((2,)),
            dma((zn, 2, CHUNKS)),
            dma((2, cols_n, CHUNKS)),
            dma((rows_n,)),
            dma((zn, CHUNKS)),
            dma((zn, CHUNKS)),
            dma((2, CHUNKS)),
            dma((zn, CHUNKS)),
            dma((2, yn, CHUNKS)),
            dma((2, yn, CHUNKS)),
            dma((rows_n,)),
        ],
        compiler_params=pltpu.CompilerParams(
            collective_id=0, has_side_effects=True, vmem_limit_bytes=2 * words + (8 << 20)
        ),
        cost_estimate=pl.CostEstimate(
            flops=2 * group * length * width * rows_n,
            bytes_accessed=2 * rows_n * group * length,
            transcendentals=0,
        ),
    )(*(pltpu.with_memory_space_constraint(a, pltpu.HBM) for a in (density, pattern)))
    return jnp.transpose(out, (1, 0, 2))


def solution(mesh):
    return jax.shard_map(
        local,
        mesh=mesh,
        in_specs=(P(("row", "col"), None), P(("row", "col"), None)),
        out_specs=P("row", None, "col"),
        check_vma=False,
    )
```

```python
import functools

import jax
import jax.numpy as jnp
from jax import lax
from jax.experimental import pallas as pl
from jax.experimental.pallas import tpu as pltpu
from jax.sharding import PartitionSpec as P

MESH = pl.DeviceIdType.MESH
CHUNKS = 4
HALF = CHUNKS // 2
LAST = CHUNKS - 1


def kernel(
    rows_n, cols_n, dens_hbm, pat_hbm, ob, dens, pat, rowb, gb, pb, s_in,
    r_row, r_gb, r_tw, r_ob, s_up, s_dn, s_dup, s_x, s_y, s_c, s_p,
):
    fetch_dens = pltpu.make_async_copy(dens_hbm, dens, s_in.at[0])
    fetch_pat = pltpu.make_async_copy(pat_hbm, pat, s_in.at[1])
    fetch_dens.start()
    fetch_pat.start()
    zn, yn = rows_n // 2, cols_n // 2
    length, width = dens.shape
    group = cols_n * length
    part = length // CHUNKS
    half_span = rows_n // 4
    g, c = lax.axis_index("row"), lax.axis_index("col")
    z, x = g // 2, lax.rem(g, 2)
    y, k = c // 2, lax.rem(c, 2)
    low, high = z == 0, z == zn - 1
    edge = low | high
    inner = jnp.logical_not(edge)
    proxy = (z == 1) | (z == zn - 2)
    away = jnp.where((z == 1) | low, 1, jnp.where((z == zn - 2) | high, -1, 1))
    inward = z + away
    ze = z - away

    def row_of(zz, xx):
        return zz * 2 + xx

    def when(cond, action):
        pl.when(cond)(action)

    def dev_z(zz):
        return (row_of(zz, x), c)

    dev_x = (row_of(z, 1 - x), c)
    dev_k = (g, y * 2 + 1 - k)

    def dev_y(d):
        return (g, lax.rem(y + d, yn) * 2 + k)

    barrier = pltpu.get_barrier_semaphore()

    def greet(device):
        pl.semaphore_signal(barrier, inc=1, device_id=device, device_id_type=MESH)

    greet(dev_x)
    greet(dev_k)
    for d in range(1, yn):
        greet(dev_y(d))
    when(z > 0, lambda: greet(dev_z(z - 1)))
    when(z < zn - 1, lambda: greet(dev_z(z + 1)))

    def rows_at(xx, n):
        return pl.ds(pl.multiple_of(xx * length + n * part, part), part)

    side = length // 2

    def gb_half(cc, h):
        return pl.ds(pl.multiple_of(cc * length + h * side, side), side)

    def gb_panel(cc):
        return pl.ds(pl.multiple_of(cc * length, length), length)

    blocks = pat.shape[0]
    size = length // blocks
    c0 = pl.multiple_of(c * length, length)
    x0 = pl.multiple_of(x * length, length)
    fetch_dens.wait()
    fetch_pat.wait()
    for b in range(blocks):
        for kb in range(pat.shape[1]):
            here = dens[b * size:(b + 1) * size, kb * size:(kb + 1) * size]
            keep = jnp.broadcast_to(pat[b:b + 1, kb:kb + 1], here.shape) != 0
            kept = jnp.where(keep, here.astype(jnp.float32), 0.0).astype(here.dtype)
            rowb[z, pl.ds(x0 + b * size, size), kb * size:(kb + 1) * size] = kept
            gb[0, pl.ds(c0 + b * size, size), kb * size:(kb + 1) * size] = kept

    def remote(src, dst, send, recv, device):
        return pltpu.make_async_remote_copy(
            src_ref=src, dst_ref=dst, send_sem=send, recv_sem=recv,
            device_id=device, device_id_type=MESH,
        )

    def row_copy(zz, xx, n, send, device):
        ref = rowb.at[zz, rows_at(xx, n)]
        return remote(ref, ref, send, r_row.at[zz, xx, n], device)

    def up(zz, n):
        return row_copy(zz, x, n, s_up.at[zz, n], dev_z(z + 1))

    def down(zz, n):
        return row_copy(zz, x, n, s_dn.at[zz, n], dev_z(z - 1))

    def double(zz, n):
        return row_copy(zz, 1 - x, n, s_dup.at[jnp.where(zz == z, 0, 1), n], dev_z(inward))

    def across(zz, n):
        return row_copy(zz, x, n, s_x.at[zz, n], dev_x)

    def sideways(p, d, h):
        if p == 0:
            src = gb.at[0, gb_half(c, h)]
        else:
            src = rowb.at[ze, pl.ds(pl.multiple_of(x * length + h * side, side), side)]
        return remote(
            src, gb.at[p, gb_half(c, h)], s_y.at[p, d, h], r_gb.at[p, c, h], dev_y(d)
        )

    def to_twin(p, d):
        cc = lax.rem(y + d, yn) * 2 + k
        if p == 1 and d == 0:
            src = rowb.at[ze, pl.ds(x0, length)]
        else:
            src = gb.at[p, gb_panel(cc)]
        return remote(src, gb.at[p, gb_panel(cc)], s_c.at[p, d], r_tw.at[p, cc], dev_k)

    def got_row(zz, xx, n):
        row_copy(zz, xx, n, s_dup.at[0, n], dev_x).wait_recv()

    def got_side(p, d, h):
        cc = lax.rem(y + d, yn) * 2 + k
        ref = gb.at[p, gb_half(cc, h)]
        remote(ref, ref, s_dup.at[0, 0], r_gb.at[p, cc, h], dev_x).wait_recv()

    def got_twin(p, d):
        cc = lax.rem(y + d, yn) * 2 + 1 - k
        ref = gb.at[p, gb_panel(cc)]
        remote(ref, ref, s_dup.at[0, 0], r_tw.at[p, cc], dev_x).wait_recv()

    def own_sideways(h, do):
        for d in range(1, yn):
            do(sideways(0, d, h))

    def own_sends(n, do):
        if n < HALF:
            do(across(z, n))
        else:
            when(jnp.logical_not(proxy), lambda: do(across(z, n)))
        when(z < zn - 1, lambda: do(up(z, n)))
        when(z > 0, lambda: do(down(z, n)))
        if n == CHUNKS - 1:
            do(to_twin(0, 0))

    def y_arrivals(p, do, wait):
        for d in range(1, yn):
            if wait:
                for h in range(2):
                    got_side(p, d, h)
            do(to_twin(p, d))

    def relay(zz, n, do):
        @pl.when((zz < z) & (z + 1 <= zn - 2))
        def _():
            do(up(zz, n))

        @pl.when((zz > z) & (z - 1 >= 1))
        def _():
            do(down(zz, n))

        dist = jnp.abs(zz - z)
        twice = ((zz == 0) | (zz == zn - 1)) & (
            (dist == 1) | ((dist == 2) & (n >= LAST))
        )

        @pl.when(jnp.logical_not(twice))
        def _():
            do(across(zz, n))

        adjacent = proxy & (zz == ze)

        @pl.when(adjacent)
        def _():
            if n % HALF == HALF - 1:
                for d in range(1, yn):
                    do(sideways(1, d, n // HALF))
            if n == CHUNKS - 1:
                do(to_twin(1, 0))

    def inside(zz):
        return (zz >= 0) & (zz <= zn - 1)

    def start(copy):
        copy.start()

    def finish(copy):
        copy.wait_send()

    step_rows = 2 * length

    def product(p, block, panel, store):
        at = pl.ds(pl.multiple_of(block * step_rows, step_rows), step_rows)
        store(at, lax.dot_general(
            gb[p, at, :], panel[...], (((1,), (1,)), ((), ())),
            preferred_element_type=jnp.float32,
        ).astype(ob.dtype))

    def slot_of(gg, q):
        return lax.rem(gg + half_span - q + rows_n, rows_n)

    def own_job(zz):
        slots = [slot_of(g, row_of(zz, xx)) for xx in range(2)]

        def store(at, value):
            for xx in range(2):
                ob[slots[xx], at, :] = value[:, xx * length:(xx + 1) * length]

        def body(i, carry):
            product(0, i, rowb.at[zz], store)
            return carry

        lax.fori_loop(0, yn, body, 0)

    def proxy_copy(q, block):
        s = slot_of(row_of(ze, x), q)
        at = pl.ds(pl.multiple_of(block * step_rows, step_rows), step_rows)
        return remote(
            pb.at[q, at], ob.at[s, at], s_p.at[q, block], r_ob.at[s, block], dev_z(ze)
        )

    def proxy_job(zz, xx, low_d, high_d):
        q = row_of(zz, xx)

        def store(at, value):
            pb[q, at, :] = value

        def body(d, carry):
            block = lax.rem(y + d, yn)
            panel = rowb.at[zz, pl.ds(pl.multiple_of(xx * length, length), length)]
            product(1, block, panel, store)
            proxy_copy(q, block).start()
            return carry

        lax.fori_loop(low_d, high_d, body, 0)

    neighbours = 2 + (yn - 1)
    pl.semaphore_wait(barrier, neighbours + jnp.where(edge, 1, 2))

    for n in range(CHUNKS):
        own_sends(n, start)

        if n == HALF - 1:
            own_sideways(0, start)
        if n == CHUNKS - 1:
            when(edge, lambda: own_sideways(1, start))

    @pl.when(edge)
    def _():
        for n in range(CHUNKS):
            got_row(z, 1 - x, n)
            double(z, n).start()
            got_row(inward, x, n)
            across(inward, n).start()
        y_arrivals(0, start, True)
        for d in range(yn):
            got_twin(0, d)

        def job(j, carry):
            @pl.when(j == 1)
            def _():
                for n in range(CHUNKS):
                    got_row(inward, 1 - x, n)
                    if n >= HALF:
                        double(inward, n).start()

            own_job(jnp.where(j == 0, z, inward))
            return carry

        lax.fori_loop(0, 2, job, 0)

        for n in range(CHUNKS):
            own_sends(n, finish)
            double(z, n).wait_send()
            across(inward, n).wait_send()
            if n >= HALF:
                double(inward, n).wait_send()
        own_sideways(0, finish)
        own_sideways(1, finish)
        y_arrivals(0, finish, False)

        def far(i, carry):
            zz = inward + away * (i // 2 + 1)
            xx = jnp.where(lax.rem(i, 2) == 0, x, 1 - x)
            s = slot_of(g, row_of(zz, xx))
            for d in range(yn):
                block = lax.rem(y + d, yn)
                at = pl.ds(pl.multiple_of(block * step_rows, step_rows), step_rows)
                ref = ob.at[s, at]
                remote(ref, ref, s_p.at[0, 0], r_ob.at[s, block], dev_x).wait_recv()
            return carry

        lax.fori_loop(0, 2 * (zn - 2), far, 0)

    @pl.when(inner)
    def _():
        def settle():
            for n in range(CHUNKS):
                own_sends(n, finish)
            own_sideways(0, finish)
            own_sideways(1, finish)
            y_arrivals(0, finish, False)

            @pl.when(proxy)
            def _():
                y_arrivals(1, finish, False)
                for n in range(LAST, CHUNKS):
                    double(ze, n).wait_send()

            def relayed(zz, carry):
                @pl.when(zz != z)
                def _():
                    for n in range(CHUNKS):
                        relay(zz, n, finish)

                return carry

            lax.fori_loop(0, zn, relayed, 0)

        def turn(t, carry):
            first, second = t == 1, t == 2

            @pl.when(t == zn - 1)
            def _():
                settle()


            def forwards(n):
                for zz in (z - t * away, z + t * away):
                    @pl.when(inside(zz))
                    def _():
                        got_row(zz, x, n)
                        relay(zz, n, start)

                @pl.when(second & proxy)
                def _():
                    got_row(ze, 1 - x, n)
                    if n >= LAST:
                        double(ze, n).start()

            def proxied(dist, xx, low_d=0, high_d=yn):
                @pl.when(proxy & (dist >= 1) & inside(z + dist * away))
                def _():
                    proxy_job(z + dist * away, xx, low_d, high_d)

            def got_other(zz):
                @pl.when(inside(zz) & jnp.logical_not(proxy & (zz == ze)))
                def _():
                    for n in range(CHUNKS):
                        got_row(zz, 1 - x, n)

            for n in range(HALF):
                forwards(n)

            @pl.when(second & proxy)
            def _():
                y_arrivals(1, start, True)
                for d in range(1, yn):
                    got_twin(1, d)
                proxied(t - 1, x, 1)

            for n in range(HALF, CHUNKS):
                if n == LAST:
                    @pl.when(t > 1)
                    def _():
                        got_other(z + (t - 1) * away)
                        proxied(t - 1, 1 - x)
                forwards(n)

            @pl.when(first)
            def _():
                own_sideways(1, start)

            @pl.when(first & proxy)
            def _():
                gb[1, pl.ds(c0, length), :] = rowb[ze, pl.ds(x0, length), :]
                got_twin(1, 0)
                proxied(t, x, 0, 1)

            @pl.when(t > 1)
            def _():
                proxied(t, x)
                got_other(z - (t - 1) * away)

            @pl.when(second)
            def _():
                y_arrivals(0, start, True)
                for d in range(yn):
                    got_twin(0, d)

            def own(j, inner_carry):
                zz = z + jnp.where(j == 0, 1 - t, jnp.where(j == 1, t - 1, 0)) * away
                last = j == 2

                @pl.when(last & (t == zn - 1))
                def _():
                    for n in range(CHUNKS):
                        got_row(z, 1 - x, n)

                @pl.when(inside(zz) & (jnp.logical_not(last) | (t == zn - 1)))
                def _():
                    own_job(zz)

                return inner_carry

            @pl.when(t > 1)
            def _():
                lax.fori_loop(0, 3, own, 0)

            return carry

        lax.fori_loop(1, zn, turn, 0)

        @pl.when(proxy)
        def _():
            def sent(i, carry):
                zz = z + away * (i // 2 + 1)
                for d in range(yn):
                    proxy_copy(row_of(zz, lax.rem(i, 2)), d).wait_send()
                return carry

            lax.fori_loop(0, 2 * (zn - 2), sent, 0)


def local(density, pattern):
    rows_n, cols_n = lax.axis_size("row"), lax.axis_size("col")
    length, width = density.shape
    group = cols_n * length
    zn, yn = rows_n // 2, cols_n // 2
    kind = density.dtype
    dma = pltpu.SemaphoreType.DMA
    words = (2 * rows_n * group * length + (2 * group + rows_n * length + 2 * length) * width)
    out = pl.pallas_call(
        functools.partial(kernel, rows_n, cols_n),
        out_shape=jax.ShapeDtypeStruct((rows_n, group, length), kind),
        in_specs=[pl.BlockSpec(memory_space=pltpu.HBM)] * 2,
        out_specs=pl.BlockSpec(memory_space=pltpu.VMEM),
        scratch_shapes=[
            pltpu.VMEM((length, width), kind),
            pltpu.VMEM(pattern.shape, pattern.dtype),
            pltpu.VMEM((zn, 2 * length, width), kind),
            pltpu.VMEM((2, group, width), kind),
            pltpu.VMEM((rows_n, group, length), kind),
            dma((2,)),
            dma((zn, 2, CHUNKS)),
            dma((2, cols_n, 2)),
            dma((2, cols_n)),
            dma((rows_n, yn)),
            dma((zn, CHUNKS)),
            dma((zn, CHUNKS)),
            dma((2, CHUNKS)),
            dma((zn, CHUNKS)),
            dma((2, yn, 2)),
            dma((2, yn)),
            dma((rows_n, yn)),
        ],
        compiler_params=pltpu.CompilerParams(
            collective_id=0, has_side_effects=True, vmem_limit_bytes=2 * words + (8 << 20)
        ),
        cost_estimate=pl.CostEstimate(
            flops=2 * group * length * width * rows_n,
            bytes_accessed=2 * rows_n * group * length,
            transcendentals=0,
        ),
    )(*(pltpu.with_memory_space_constraint(a, pltpu.HBM) for a in (density, pattern)))
    return jnp.transpose(out, (1, 0, 2))


def solution(mesh):
    return jax.shard_map(
        local,
        mesh=mesh,
        in_specs=(P(("row", "col"), None), P(("row", "col"), None)),
        out_specs=P("row", None, "col"),
        check_vma=False,
    )
```

```python
import functools

import jax
import jax.numpy as jnp
from jax import lax
from jax.experimental import pallas as pl
from jax.experimental.pallas import tpu as pltpu
from jax.sharding import PartitionSpec as P

MESH = pl.DeviceIdType.MESH
CHUNKS = 8
HALF = CHUNKS // 2
LAST = CHUNKS * 3 // 4
EARLY = CHUNKS // 4
LAG = 3

def kernel(
    rows_n, cols_n, dens_hbm, pat_hbm, ob, dens, pat, rowb, gb, pb, s_in,
    r_row, r_gb, r_tw, r_ob, s_up, s_dn, s_dup, s_x, s_y, s_c, s_p,
):
    fetch_dens = pltpu.make_async_copy(dens_hbm, dens, s_in.at[0])
    fetch_pat = pltpu.make_async_copy(pat_hbm, pat, s_in.at[1])
    fetch_dens.start()
    fetch_pat.start()
    zn, yn = rows_n // 2, cols_n // 2
    length, width = dens.shape
    group = cols_n * length
    part = length // CHUNKS
    half_span = rows_n // 4
    g, c = lax.axis_index("row"), lax.axis_index("col")
    z, x = g // 2, lax.rem(g, 2)
    y, k = c // 2, lax.rem(c, 2)
    low, high = z == 0, z == zn - 1
    edge = low | high
    inner = jnp.logical_not(edge)
    proxy = (z == 1) | (z == zn - 2)
    away = jnp.where((z == 1) | low, 1, jnp.where((z == zn - 2) | high, -1, 1))
    inward = z + away
    ze = z - away

    def row_of(zz, xx):
        return zz * 2 + xx

    def when(cond, action):
        pl.when(cond)(action)

    def dev_z(zz):
        return (row_of(zz, x), c)

    dev_x = (row_of(z, 1 - x), c)
    dev_k = (g, y * 2 + 1 - k)

    def dev_y(d):
        return (g, lax.rem(y + d, yn) * 2 + k)

    barrier = pltpu.get_barrier_semaphore()

    def greet(device):
        pl.semaphore_signal(barrier, inc=1, device_id=device, device_id_type=MESH)

    greet(dev_x)
    greet(dev_k)
    for d in range(1, yn):
        greet(dev_y(d))
    when(z > 0, lambda: greet(dev_z(z - 1)))
    when(z < zn - 1, lambda: greet(dev_z(z + 1)))

    def rows_at(xx, n):
        return pl.ds(pl.multiple_of(xx * length + n * part, part), part)

    def gb_rows(cc, n):
        return pl.ds(pl.multiple_of(cc * length + n * part, part), part)

    def gb_panel(cc):
        return pl.ds(pl.multiple_of(cc * length, length), length)

    blocks = pat.shape[0]
    size = length // blocks
    c0 = pl.multiple_of(c * length, length)
    x0 = pl.multiple_of(x * length, length)
    fetch_dens.wait()
    fetch_pat.wait()
    for b in range(blocks):
        for kb in range(pat.shape[1]):
            here = dens[b * size:(b + 1) * size, kb * size:(kb + 1) * size]
            keep = jnp.broadcast_to(pat[b:b + 1, kb:kb + 1], here.shape) != 0
            kept = jnp.where(keep, here.astype(jnp.float32), 0.0).astype(here.dtype)
            rowb[z, pl.ds(x0 + b * size, size), kb * size:(kb + 1) * size] = kept
            gb[0, pl.ds(c0 + b * size, size), kb * size:(kb + 1) * size] = kept

    def remote(src, dst, send, recv, device):
        return pltpu.make_async_remote_copy(
            src_ref=src, dst_ref=dst, send_sem=send, recv_sem=recv,
            device_id=device, device_id_type=MESH,
        )

    def row_copy(zz, xx, n, send, device):
        ref = rowb.at[zz, rows_at(xx, n)]
        return remote(ref, ref, send, r_row.at[zz, xx, n], device)

    def up(zz, n):
        return row_copy(zz, x, n, s_up.at[zz, n], dev_z(z + 1))

    def down(zz, n):
        return row_copy(zz, x, n, s_dn.at[zz, n], dev_z(z - 1))

    def double(zz, n):
        return row_copy(zz, 1 - x, n, s_dup.at[jnp.where(zz == z, 0, 1), n], dev_z(inward))

    def across(zz, n):
        return row_copy(zz, x, n, s_x.at[zz, n], dev_x)

    def sideways(p, d, n):
        src = gb.at[0, gb_rows(c, n)] if p == 0 else rowb.at[ze, rows_at(x, n)]
        return remote(
            src, gb.at[p, gb_rows(c, n)], s_y.at[p, d, n], r_gb.at[p, c, n], dev_y(d)
        )

    def to_twin(d):
        cc = lax.rem(y + d, yn) * 2 + k
        ref = gb.at[0, gb_panel(cc)]
        return remote(ref, ref, s_c.at[0, d, 0], r_tw.at[0, cc, 0], dev_k)

    def edge_to_twin(d, n):
        cc = lax.rem(y + d, yn) * 2 + k
        dst = gb.at[1, gb_rows(cc, n)]
        src = rowb.at[ze, rows_at(x, n)] if d == 0 else dst
        return remote(src, dst, s_c.at[1, d, n], r_tw.at[1, cc, n], dev_k)

    def got_row(zz, xx, n):
        row_copy(zz, xx, n, s_dup.at[0, n], dev_x).wait_recv()

    def got_side(p, d, n):
        cc = lax.rem(y + d, yn) * 2 + k
        ref = gb.at[p, gb_rows(cc, n)]
        remote(ref, ref, s_dup.at[0, 0], r_gb.at[p, cc, n], dev_x).wait_recv()

    def got_twin(d):
        cc = lax.rem(y + d, yn) * 2 + 1 - k
        ref = gb.at[0, gb_panel(cc)]
        remote(ref, ref, s_dup.at[0, 0], r_tw.at[0, cc, 0], dev_x).wait_recv()

    def got_edge_twin(d):
        cc = lax.rem(y + d, yn) * 2 + 1 - k
        for n in range(CHUNKS):
            ref = gb.at[1, gb_rows(cc, n)]
            remote(ref, ref, s_dup.at[0, 0], r_tw.at[1, cc, n], dev_x).wait_recv()

    def own_sideways(chunks, do):
        for d in range(1, yn):
            for n in chunks:
                do(sideways(0, d, n))

    def own_sends(n, do):
        if n < HALF:
            do(across(z, n))
        else:
            when(jnp.logical_not(proxy), lambda: do(across(z, n)))
        when(z < zn - 1, lambda: do(up(z, n)))
        when(z > 0, lambda: do(down(z, n)))
        if n == CHUNKS - 1:
            do(to_twin(0))

    def y_arrivals(do, wait):
        for d in range(1, yn):
            if wait:
                for n in range(CHUNKS):
                    got_side(0, d, n)
            do(to_twin(d))

    def edge_arrivals(n, do, wait):
        for d in range(1, yn):
            if wait:
                got_side(1, d, n)
            do(edge_to_twin(d, n))

    def relay(zz, n, do):
        @pl.when((zz < z) & (z + 1 <= zn - 2))
        def _():
            do(up(zz, n))

        @pl.when((zz > z) & (z - 1 >= 1))
        def _():
            do(down(zz, n))

        dist = jnp.abs(zz - z)
        twice = ((zz == 0) | (zz == zn - 1)) & (
            (dist == 1) | ((dist == 2) & (n >= LAST))
        )

        @pl.when(jnp.logical_not(twice))
        def _():
            do(across(zz, n))

        adjacent = proxy & (zz == ze)

        @pl.when(adjacent)
        def _():
            for d in range(1, yn):
                do(sideways(1, d, n))
            do(edge_to_twin(0, n))

    def inside(zz):
        return (zz >= 0) & (zz <= zn - 1)

    def start(copy):
        copy.start()

    def finish(copy):
        copy.wait_send()

    step_rows = 2 * length

    def product(p, block, panel, store):
        at = pl.ds(pl.multiple_of(block * step_rows, step_rows), step_rows)
        store(at, lax.dot_general(
            gb[p, at, :], panel[...], (((1,), (1,)), ((), ())),
            preferred_element_type=jnp.float32,
        ).astype(ob.dtype))

    def slot_of(gg, q):
        return lax.rem(gg + half_span - q + rows_n, rows_n)

    def own_job(zz):
        slots = [slot_of(g, row_of(zz, xx)) for xx in range(2)]

        def store(at, value):
            for xx in range(2):
                ob[slots[xx], at, :] = value[:, xx * length:(xx + 1) * length]

        def body(i, carry):
            product(0, i, rowb.at[zz], store)
            return carry

        lax.fori_loop(0, yn, body, 0)

    def proxy_copy(q, block):
        s = slot_of(row_of(ze, x), q)
        at = pl.ds(pl.multiple_of(block * step_rows, step_rows), step_rows)
        return remote(
            pb.at[q, at], ob.at[s, at], s_p.at[q, block], r_ob.at[s, block], dev_z(ze)
        )

    def proxy_job(zz, xx, low_d, high_d):
        q = row_of(zz, xx)

        def store(at, value):
            pb[q, at, :] = value

        def body(d, carry):
            block = lax.rem(y + d, yn)
            panel = rowb.at[zz, pl.ds(pl.multiple_of(xx * length, length), length)]
            product(1, block, panel, store)
            proxy_copy(q, block).start()
            return carry

        lax.fori_loop(low_d, high_d, body, 0)

    neighbours = 2 + (yn - 1)
    pl.semaphore_wait(barrier, neighbours + jnp.where(edge, 1, 2))

    for n in range(CHUNKS):
        own_sends(n, start)

        if n < EARLY:
            own_sideways([n], start)
        else:
            when(edge, functools.partial(own_sideways, [n], start))

    @pl.when(edge)
    def _():
        for n in range(CHUNKS):
            got_row(z, 1 - x, n)
            double(z, n).start()
            got_row(inward, x, n)
            across(inward, n).start()
        y_arrivals(start, True)
        for d in range(yn):
            got_twin(d)

        def job(j, carry):
            @pl.when(j == 1)
            def _():
                for n in range(CHUNKS):
                    got_row(inward, 1 - x, n)
                    if n >= HALF:
                        double(inward, n).start()

            own_job(jnp.where(j == 0, z, inward))
            return carry

        lax.fori_loop(0, 2, job, 0)

        for n in range(CHUNKS):
            own_sends(n, finish)
            double(z, n).wait_send()
            across(inward, n).wait_send()
            if n >= HALF:
                double(inward, n).wait_send()
        own_sideways(range(CHUNKS), finish)
        y_arrivals(finish, False)

        def far(i, carry):
            zz = inward + away * (i // 2 + 1)
            xx = jnp.where(lax.rem(i, 2) == 0, x, 1 - x)
            s = slot_of(g, row_of(zz, xx))
            for d in range(yn):
                block = lax.rem(y + d, yn)
                at = pl.ds(pl.multiple_of(block * step_rows, step_rows), step_rows)
                ref = ob.at[s, at]
                remote(ref, ref, s_p.at[0, 0], r_ob.at[s, block], dev_x).wait_recv()
            return carry

        lax.fori_loop(0, 2 * (zn - 2), far, 0)

    @pl.when(inner)
    def _():
        def settle():
            for n in range(CHUNKS):
                own_sends(n, finish)
            own_sideways(range(CHUNKS), finish)
            y_arrivals(finish, False)

            @pl.when(proxy)
            def _():
                for n in range(CHUNKS):
                    edge_arrivals(n, finish, False)
                for n in range(LAST, CHUNKS):
                    double(ze, n).wait_send()

            def relayed(zz, carry):
                @pl.when(zz != z)
                def _():
                    for n in range(CHUNKS):
                        relay(zz, n, finish)

                return carry

            lax.fori_loop(0, zn, relayed, 0)

        def turn(t, carry):
            first, second = t == 1, t == 2

            @pl.when(t == zn - 1)
            def _():
                settle()

            def forwards(n):
                for zz in (z - t * away, z + t * away):
                    @pl.when(inside(zz))
                    def _():
                        got_row(zz, x, n)
                        relay(zz, n, start)

                @pl.when(second & proxy)
                def _():
                    got_row(ze, 1 - x, n)
                    if n >= LAST:
                        double(ze, n).start()

            def proxied(dist, xx, low_d=0, high_d=yn):
                @pl.when(proxy & (dist >= 1) & inside(z + dist * away))
                def _():
                    proxy_job(z + dist * away, xx, low_d, high_d)

            def got_other(zz):
                @pl.when(inside(zz) & jnp.logical_not(proxy & (zz == ze)))
                def _():
                    for n in range(CHUNKS):
                        got_row(zz, 1 - x, n)

            for n in range(CHUNKS):
                if n == HALF:
                    @pl.when(t > 1)
                    def _():
                        got_other(z + (t - 1) * away)
                        proxied(t - 1, 1 - x)
                forwards(n)
                if n >= LAG:
                    @pl.when(first & proxy)
                    def _():
                        edge_arrivals(n - LAG, start, True)

            @pl.when(first)
            def _():
                own_sideways(range(EARLY, CHUNKS), start)

            @pl.when(first & proxy)
            def _():
                gb[1, pl.ds(c0, length), :] = rowb[ze, pl.ds(x0, length), :]
                got_edge_twin(0)
                proxied(t, x, 0, 1)
                for n in range(CHUNKS - LAG, CHUNKS):
                    edge_arrivals(n, start, True)
                for d in range(1, yn):
                    got_edge_twin(d)
                proxied(t, x, 1)

            @pl.when(t > 1)
            def _():
                proxied(t, x)
                got_other(z - (t - 1) * away)

            @pl.when(second)
            def _():
                y_arrivals(start, True)
                for d in range(yn):
                    got_twin(d)

            def own(j, inner_carry):
                zz = z + jnp.where(j == 0, 1 - t, jnp.where(j == 1, t - 1, 0)) * away
                last = j == 2

                @pl.when(last & (t == zn - 1))
                def _():
                    for n in range(CHUNKS):
                        got_row(z, 1 - x, n)

                @pl.when(inside(zz) & (jnp.logical_not(last) | (t == zn - 1)))
                def _():
                    own_job(zz)

                return inner_carry

            @pl.when(t > 1)
            def _():
                lax.fori_loop(0, 3, own, 0)

            return carry

        lax.fori_loop(1, zn, turn, 0)

        @pl.when(proxy)
        def _():
            def sent(i, carry):
                zz = z + away * (i // 2 + 1)
                for d in range(yn):
                    proxy_copy(row_of(zz, lax.rem(i, 2)), d).wait_send()
                return carry

            lax.fori_loop(0, 2 * (zn - 2), sent, 0)


def local(density, pattern):
    rows_n, cols_n = lax.axis_size("row"), lax.axis_size("col")
    length, width = density.shape
    group = cols_n * length
    zn, yn = rows_n // 2, cols_n // 2
    kind = density.dtype
    dma = pltpu.SemaphoreType.DMA
    words = (2 * rows_n * group * length + (2 * group + rows_n * length + 2 * length) * width)
    out = pl.pallas_call(
        functools.partial(kernel, rows_n, cols_n),
        out_shape=jax.ShapeDtypeStruct((rows_n, group, length), kind),
        in_specs=[pl.BlockSpec(memory_space=pltpu.HBM)] * 2,
        out_specs=pl.BlockSpec(memory_space=pltpu.VMEM),
        scratch_shapes=[
            pltpu.VMEM((length, width), kind),
            pltpu.VMEM(pattern.shape, pattern.dtype),
            pltpu.VMEM((zn, 2 * length, width), kind),
            pltpu.VMEM((2, group, width), kind),
            pltpu.VMEM((rows_n, group, length), kind),
            dma((2,)),
            dma((zn, 2, CHUNKS)),
            dma((2, cols_n, CHUNKS)),
            dma((2, cols_n, CHUNKS)),
            dma((rows_n, yn)),
            dma((zn, CHUNKS)),
            dma((zn, CHUNKS)),
            dma((2, CHUNKS)),
            dma((zn, CHUNKS)),
            dma((2, yn, CHUNKS)),
            dma((2, yn, CHUNKS)),
            dma((rows_n, yn)),
        ],
        compiler_params=pltpu.CompilerParams(
            collective_id=0, has_side_effects=True, vmem_limit_bytes=2 * words + (8 << 20)
        ),
        cost_estimate=pl.CostEstimate(
            flops=2 * group * length * width * rows_n,
            bytes_accessed=2 * rows_n * group * length,
            transcendentals=0,
        ),
    )(*(pltpu.with_memory_space_constraint(a, pltpu.HBM) for a in (density, pattern)))
    return jnp.transpose(out, (1, 0, 2))


def solution(mesh):
    return jax.shard_map(
        local,
        mesh=mesh,
        in_specs=(P(("row", "col"), None), P(("row", "col"), None)),
        out_specs=P("row", None, "col"),
        check_vma=False,
    )
```

```python
import functools

import jax
import jax.numpy as jnp
from jax import lax
from jax.experimental import pallas as pl
from jax.experimental.pallas import tpu as pltpu
from jax.sharding import PartitionSpec as P

MESH = pl.DeviceIdType.MESH
CHUNKS = 4
HALF = CHUNKS // 2
LAST = CHUNKS * 3 // 4
EARLY = CHUNKS // 4
LAG = 2

def kernel(
    rows_n, cols_n, dens_hbm, pat_hbm, ob, dens, pat, rowb, gb, pb, s_in,
    r_row, r_gb, r_tw, r_ob, s_up, s_dn, s_dup, s_x, s_y, s_c, s_p,
):
    fetch_dens = pltpu.make_async_copy(dens_hbm, dens, s_in.at[0])
    fetch_pat = pltpu.make_async_copy(pat_hbm, pat, s_in.at[1])
    fetch_dens.start()
    fetch_pat.start()
    zn, yn = rows_n // 2, cols_n // 2
    length, width = dens.shape
    group = cols_n * length
    part = length // CHUNKS
    half_span = rows_n // 4
    g, c = lax.axis_index("row"), lax.axis_index("col")
    z, x = g // 2, lax.rem(g, 2)
    y, k = c // 2, lax.rem(c, 2)
    low, high = z == 0, z == zn - 1
    edge = low | high
    inner = jnp.logical_not(edge)
    proxy = (z == 1) | (z == zn - 2)
    away = jnp.where((z == 1) | low, 1, jnp.where((z == zn - 2) | high, -1, 1))
    inward = z + away
    ze = z - away

    def row_of(zz, xx):
        return zz * 2 + xx

    def when(cond, action):
        pl.when(cond)(action)

    def dev_z(zz):
        return (row_of(zz, x), c)

    dev_x = (row_of(z, 1 - x), c)
    dev_k = (g, y * 2 + 1 - k)

    def dev_y(d):
        return (g, lax.rem(y + d, yn) * 2 + k)

    barrier = pltpu.get_barrier_semaphore()

    def greet(device):
        pl.semaphore_signal(barrier, inc=1, device_id=device, device_id_type=MESH)

    greet(dev_x)
    greet(dev_k)
    for d in range(1, yn):
        greet(dev_y(d))
    when(z > 0, lambda: greet(dev_z(z - 1)))
    when(z < zn - 1, lambda: greet(dev_z(z + 1)))

    def rows_at(xx, n):
        return pl.ds(pl.multiple_of(xx * length + n * part, part), part)

    def gb_rows(cc, n):
        return pl.ds(pl.multiple_of(cc * length + n * part, part), part)

    def gb_panel(cc):
        return pl.ds(pl.multiple_of(cc * length, length), length)

    blocks = pat.shape[0]
    size = length // blocks
    c0 = pl.multiple_of(c * length, length)
    x0 = pl.multiple_of(x * length, length)
    fetch_dens.wait()
    fetch_pat.wait()
    for b in range(blocks):
        for kb in range(pat.shape[1]):
            here = dens[b * size:(b + 1) * size, kb * size:(kb + 1) * size]
            keep = jnp.broadcast_to(pat[b:b + 1, kb:kb + 1], here.shape) != 0
            kept = jnp.where(keep, here.astype(jnp.float32), 0.0).astype(here.dtype)
            rowb[z, pl.ds(x0 + b * size, size), kb * size:(kb + 1) * size] = kept
            gb[0, pl.ds(c0 + b * size, size), kb * size:(kb + 1) * size] = kept

    def remote(src, dst, send, recv, device):
        return pltpu.make_async_remote_copy(
            src_ref=src, dst_ref=dst, send_sem=send, recv_sem=recv,
            device_id=device, device_id_type=MESH,
        )

    def row_copy(zz, xx, n, send, device):
        ref = rowb.at[zz, rows_at(xx, n)]
        return remote(ref, ref, send, r_row.at[zz, xx, n], device)

    def up(zz, n):
        return row_copy(zz, x, n, s_up.at[zz, n], dev_z(z + 1))

    def down(zz, n):
        return row_copy(zz, x, n, s_dn.at[zz, n], dev_z(z - 1))

    def double(zz, n):
        return row_copy(zz, 1 - x, n, s_dup.at[jnp.where(zz == z, 0, 1), n], dev_z(inward))

    def across(zz, n):
        return row_copy(zz, x, n, s_x.at[zz, n], dev_x)

    def sideways(p, d, n):
        src = gb.at[0, gb_rows(c, n)] if p == 0 else rowb.at[ze, rows_at(x, n)]
        return remote(
            src, gb.at[p, gb_rows(c, n)], s_y.at[p, d, n], r_gb.at[p, c, n], dev_y(d)
        )

    def to_twin(d):
        cc = lax.rem(y + d, yn) * 2 + k
        ref = gb.at[0, gb_panel(cc)]
        return remote(ref, ref, s_c.at[0, d, 0], r_tw.at[0, cc, 0], dev_k)

    def edge_to_twin(d, n):
        cc = lax.rem(y + d, yn) * 2 + k
        dst = gb.at[1, gb_rows(cc, n)]
        src = rowb.at[ze, rows_at(x, n)] if d == 0 else dst
        return remote(src, dst, s_c.at[1, d, n], r_tw.at[1, cc, n], dev_k)

    def got_row(zz, xx, n):
        row_copy(zz, xx, n, s_dup.at[0, n], dev_x).wait_recv()

    def got_side(p, d, n):
        cc = lax.rem(y + d, yn) * 2 + k
        ref = gb.at[p, gb_rows(cc, n)]
        remote(ref, ref, s_dup.at[0, 0], r_gb.at[p, cc, n], dev_x).wait_recv()

    def got_twin(d):
        cc = lax.rem(y + d, yn) * 2 + 1 - k
        ref = gb.at[0, gb_panel(cc)]
        remote(ref, ref, s_dup.at[0, 0], r_tw.at[0, cc, 0], dev_x).wait_recv()

    def got_edge_twin(d):
        cc = lax.rem(y + d, yn) * 2 + 1 - k
        for n in range(CHUNKS):
            ref = gb.at[1, gb_rows(cc, n)]
            remote(ref, ref, s_dup.at[0, 0], r_tw.at[1, cc, n], dev_x).wait_recv()

    def own_sideways(chunks, do):
        for d in range(1, yn):
            for n in chunks:
                do(sideways(0, d, n))

    def own_sends(n, do):
        if n < HALF:
            do(across(z, n))
        else:
            when(jnp.logical_not(proxy), lambda: do(across(z, n)))
        when(z < zn - 1, lambda: do(up(z, n)))
        when(z > 0, lambda: do(down(z, n)))
        if n == CHUNKS - 1:
            do(to_twin(0))

    def y_arrivals(do, wait):
        for d in range(1, yn):
            if wait:
                for n in range(CHUNKS):
                    got_side(0, d, n)
            do(to_twin(d))

    def edge_arrivals(n, do, wait):
        for d in range(1, yn):
            if wait:
                got_side(1, d, n)
            do(edge_to_twin(d, n))

    def relay(zz, n, do):
        @pl.when((zz < z) & (z + 1 <= zn - 2))
        def _():
            do(up(zz, n))

        @pl.when((zz > z) & (z - 1 >= 1))
        def _():
            do(down(zz, n))

        dist = jnp.abs(zz - z)
        twice = ((zz == 0) | (zz == zn - 1)) & (
            (dist == 1) | ((dist == 2) & (n >= LAST))
        )

        @pl.when(jnp.logical_not(twice))
        def _():
            do(across(zz, n))

        adjacent = proxy & (zz == ze)

        @pl.when(adjacent)
        def _():
            for d in range(1, yn):
                do(sideways(1, d, n))
            do(edge_to_twin(0, n))

    def inside(zz):
        return (zz >= 0) & (zz <= zn - 1)

    def start(copy):
        copy.start()

    def finish(copy):
        copy.wait_send()

    step_rows = 2 * length

    def product(p, block, panel, store):
        at = pl.ds(pl.multiple_of(block * step_rows, step_rows), step_rows)
        store(at, lax.dot_general(
            gb[p, at, :], panel[...], (((1,), (1,)), ((), ())),
            preferred_element_type=jnp.float32,
        ).astype(ob.dtype))

    def slot_of(gg, q):
        return lax.rem(gg + half_span - q + rows_n, rows_n)

    def own_job(zz):
        slots = [slot_of(g, row_of(zz, xx)) for xx in range(2)]

        def store(at, value):
            for xx in range(2):
                ob[slots[xx], at, :] = value[:, xx * length:(xx + 1) * length]

        def body(i, carry):
            product(0, i, rowb.at[zz], store)
            return carry

        lax.fori_loop(0, yn, body, 0)

    def proxy_copy(q, block):
        s = slot_of(row_of(ze, x), q)
        at = pl.ds(pl.multiple_of(block * step_rows, step_rows), step_rows)
        return remote(
            pb.at[q, at], ob.at[s, at], s_p.at[q, block], r_ob.at[s, block], dev_z(ze)
        )

    def proxy_job(zz, xx, low_d, high_d):
        q = row_of(zz, xx)

        def store(at, value):
            pb[q, at, :] = value

        def body(d, carry):
            block = lax.rem(y + d, yn)
            panel = rowb.at[zz, pl.ds(pl.multiple_of(xx * length, length), length)]
            product(1, block, panel, store)
            proxy_copy(q, block).start()
            return carry

        lax.fori_loop(low_d, high_d, body, 0)

    neighbours = 2 + (yn - 1)
    pl.semaphore_wait(barrier, neighbours + jnp.where(edge, 1, 2))

    for n in range(CHUNKS):
        own_sends(n, start)

        if n < EARLY:
            own_sideways([n], start)
        else:
            when(edge, functools.partial(own_sideways, [n], start))

    @pl.when(edge)
    def _():
        for n in range(CHUNKS):
            got_row(z, 1 - x, n)
            double(z, n).start()
            got_row(inward, x, n)
            across(inward, n).start()
        y_arrivals(start, True)
        for d in range(yn):
            got_twin(d)

        def job(j, carry):
            @pl.when(j == 1)
            def _():
                for n in range(CHUNKS):
                    got_row(inward, 1 - x, n)
                    if n >= HALF:
                        double(inward, n).start()

            own_job(jnp.where(j == 0, z, inward))
            return carry

        lax.fori_loop(0, 2, job, 0)

        for n in range(CHUNKS):
            own_sends(n, finish)
            double(z, n).wait_send()
            across(inward, n).wait_send()
            if n >= HALF:
                double(inward, n).wait_send()
        own_sideways(range(CHUNKS), finish)
        y_arrivals(finish, False)

        def far(i, carry):
            zz = inward + away * (i // 2 + 1)
            xx = jnp.where(lax.rem(i, 2) == 0, x, 1 - x)
            s = slot_of(g, row_of(zz, xx))
            for d in range(yn):
                block = lax.rem(y + d, yn)
                at = pl.ds(pl.multiple_of(block * step_rows, step_rows), step_rows)
                ref = ob.at[s, at]
                remote(ref, ref, s_p.at[0, 0], r_ob.at[s, block], dev_x).wait_recv()
            return carry

        lax.fori_loop(0, 2 * (zn - 2), far, 0)

    @pl.when(inner)
    def _():
        def settle():
            for n in range(CHUNKS):
                own_sends(n, finish)
            own_sideways(range(CHUNKS), finish)
            y_arrivals(finish, False)

            @pl.when(proxy)
            def _():
                for n in range(CHUNKS):
                    edge_arrivals(n, finish, False)
                for n in range(LAST, CHUNKS):
                    double(ze, n).wait_send()

            def relayed(zz, carry):
                @pl.when(zz != z)
                def _():
                    for n in range(CHUNKS):
                        relay(zz, n, finish)

                return carry

            lax.fori_loop(0, zn, relayed, 0)

        def turn(t, carry):
            first, second = t == 1, t == 2

            @pl.when(t == zn - 1)
            def _():
                settle()

            def forwards(n):
                for zz in (z - t * away, z + t * away):
                    @pl.when(inside(zz))
                    def _():
                        got_row(zz, x, n)
                        relay(zz, n, start)

                @pl.when(second & proxy)
                def _():
                    got_row(ze, 1 - x, n)
                    if n >= LAST:
                        double(ze, n).start()

            def proxied(dist, xx, low_d=0, high_d=yn):
                @pl.when(proxy & (dist >= 1) & inside(z + dist * away))
                def _():
                    proxy_job(z + dist * away, xx, low_d, high_d)

            def got_other(zz):
                @pl.when(inside(zz) & jnp.logical_not(proxy & (zz == ze)))
                def _():
                    for n in range(CHUNKS):
                        got_row(zz, 1 - x, n)

            for n in range(CHUNKS):
                if n == HALF:
                    @pl.when(t > 1)
                    def _():
                        got_other(z + (t - 1) * away)
                        proxied(t - 1, 1 - x)
                forwards(n)
                if n >= LAG:
                    @pl.when(first & proxy)
                    def _():
                        edge_arrivals(n - LAG, start, True)

            @pl.when(first)
            def _():
                own_sideways(range(EARLY, CHUNKS), start)

            @pl.when(first & proxy)
            def _():
                gb[1, pl.ds(c0, length), :] = rowb[ze, pl.ds(x0, length), :]
                got_edge_twin(0)
                proxied(t, x, 0, 1)
                for n in range(CHUNKS - LAG, CHUNKS):
                    edge_arrivals(n, start, True)
                for d in range(1, yn):
                    got_edge_twin(d)
                proxied(t, x, 1)

            @pl.when(t > 1)
            def _():
                proxied(t, x)
                got_other(z - (t - 1) * away)

            @pl.when(second)
            def _():
                y_arrivals(start, True)
                for d in range(yn):
                    got_twin(d)

            def own(j, inner_carry):
                zz = z + jnp.where(j == 0, 1 - t, jnp.where(j == 1, t - 1, 0)) * away
                last = j == 2

                @pl.when(last & (t == zn - 1))
                def _():
                    for n in range(CHUNKS):
                        got_row(z, 1 - x, n)

                @pl.when(inside(zz) & (jnp.logical_not(last) | (t == zn - 1)))
                def _():
                    own_job(zz)

                return inner_carry

            @pl.when(t > 1)
            def _():
                lax.fori_loop(0, 3, own, 0)

            return carry

        lax.fori_loop(1, zn, turn, 0)

        @pl.when(proxy)
        def _():
            def sent(i, carry):
                zz = z + away * (i // 2 + 1)
                for d in range(yn):
                    proxy_copy(row_of(zz, lax.rem(i, 2)), d).wait_send()
                return carry

            lax.fori_loop(0, 2 * (zn - 2), sent, 0)


def local(density, pattern):
    rows_n, cols_n = lax.axis_size("row"), lax.axis_size("col")
    length, width = density.shape
    group = cols_n * length
    zn, yn = rows_n // 2, cols_n // 2
    kind = density.dtype
    dma = pltpu.SemaphoreType.DMA
    words = (2 * rows_n * group * length + (2 * group + rows_n * length + 2 * length) * width)
    out = pl.pallas_call(
        functools.partial(kernel, rows_n, cols_n),
        out_shape=jax.ShapeDtypeStruct((rows_n, group, length), kind),
        in_specs=[pl.BlockSpec(memory_space=pltpu.HBM)] * 2,
        out_specs=pl.BlockSpec(memory_space=pltpu.VMEM),
        scratch_shapes=[
            pltpu.VMEM((length, width), kind),
            pltpu.VMEM(pattern.shape, pattern.dtype),
            pltpu.VMEM((zn, 2 * length, width), kind),
            pltpu.VMEM((2, group, width), kind),
            pltpu.VMEM((rows_n, group, length), kind),
            dma((2,)),
            dma((zn, 2, CHUNKS)),
            dma((2, cols_n, CHUNKS)),
            dma((2, cols_n, CHUNKS)),
            dma((rows_n, yn)),
            dma((zn, CHUNKS)),
            dma((zn, CHUNKS)),
            dma((2, CHUNKS)),
            dma((zn, CHUNKS)),
            dma((2, yn, CHUNKS)),
            dma((2, yn, CHUNKS)),
            dma((rows_n, yn)),
        ],
        compiler_params=pltpu.CompilerParams(
            collective_id=0, has_side_effects=True, vmem_limit_bytes=2 * words + (8 << 20)
        ),
        cost_estimate=pl.CostEstimate(
            flops=2 * group * length * width * rows_n,
            bytes_accessed=2 * rows_n * group * length,
            transcendentals=0,
        ),
    )(*(pltpu.with_memory_space_constraint(a, pltpu.HBM) for a in (density, pattern)))
    return jnp.transpose(out, (1, 0, 2))


def solution(mesh):
    return jax.shard_map(
        local,
        mesh=mesh,
        in_specs=(P(("row", "col"), None), P(("row", "col"), None)),
        out_specs=P("row", None, "col"),
        check_vma=False,
    )
```

```python
import functools

import jax
import jax.numpy as jnp
from jax import lax
from jax.experimental import pallas as pl
from jax.experimental.pallas import tpu as pltpu
from jax.sharding import PartitionSpec as P

MESH = pl.DeviceIdType.MESH
CHUNKS = 4
HALF = CHUNKS // 2
LAST = CHUNKS * 3 // 4
EARLY = CHUNKS // 4
LAG = 2
WINDOW = 2

def kernel(
    rows_n, cols_n, dens_hbm, pat_hbm, ob, dens, pat, rowb, gb, pb, s_in,
    r_row, r_gb, r_tw, r_ob, s_up, s_dn, s_dup, s_x, s_y, s_c, s_p,
):
    fetch_dens = pltpu.make_async_copy(dens_hbm, dens, s_in.at[0])
    fetch_pat = pltpu.make_async_copy(pat_hbm, pat, s_in.at[1])
    fetch_dens.start()
    fetch_pat.start()
    zn, yn = rows_n // 2, cols_n // 2
    length, width = dens.shape
    group = cols_n * length
    part = length // CHUNKS
    half_span = rows_n // 4
    g, c = lax.axis_index("row"), lax.axis_index("col")
    z, x = g // 2, lax.rem(g, 2)
    y, k = c // 2, lax.rem(c, 2)
    low, high = z == 0, z == zn - 1
    edge = low | high
    inner = jnp.logical_not(edge)
    proxy = (z == 1) | (z == zn - 2)
    away = jnp.where((z == 1) | low, 1, jnp.where((z == zn - 2) | high, -1, 1))
    inward = z + away
    ze = z - away

    def row_of(zz, xx):
        return zz * 2 + xx

    def when(cond, action):
        pl.when(cond)(action)

    def dev_z(zz):
        return (row_of(zz, x), c)

    dev_x = (row_of(z, 1 - x), c)
    dev_k = (g, y * 2 + 1 - k)

    def dev_y(d):
        return (g, lax.rem(y + d, yn) * 2 + k)

    barrier = pltpu.get_barrier_semaphore()

    def greet(device):
        pl.semaphore_signal(barrier, inc=1, device_id=device, device_id_type=MESH)

    greet(dev_x)
    greet(dev_k)
    for d in range(1, yn):
        greet(dev_y(d))
    when(z > 0, lambda: greet(dev_z(z - 1)))
    when(z < zn - 1, lambda: greet(dev_z(z + 1)))

    def rows_at(xx, n):
        return pl.ds(pl.multiple_of(xx * length + n * part, part), part)

    def gb_rows(cc, n):
        return pl.ds(pl.multiple_of(cc * length + n * part, part), part)

    def gb_panel(cc):
        return pl.ds(pl.multiple_of(cc * length, length), length)

    blocks = pat.shape[0]
    size = length // blocks
    c0 = pl.multiple_of(c * length, length)
    x0 = pl.multiple_of(x * length, length)
    fetch_dens.wait()
    fetch_pat.wait()
    for b in range(blocks):
        for kb in range(pat.shape[1]):
            here = dens[b * size:(b + 1) * size, kb * size:(kb + 1) * size]
            keep = jnp.broadcast_to(pat[b:b + 1, kb:kb + 1], here.shape) != 0
            kept = jnp.where(keep, here.astype(jnp.float32), 0.0).astype(here.dtype)
            rowb[z, pl.ds(x0 + b * size, size), kb * size:(kb + 1) * size] = kept
            gb[0, pl.ds(c0 + b * size, size), kb * size:(kb + 1) * size] = kept

    def remote(src, dst, send, recv, device):
        return pltpu.make_async_remote_copy(
            src_ref=src, dst_ref=dst, send_sem=send, recv_sem=recv,
            device_id=device, device_id_type=MESH,
        )

    def row_copy(zz, xx, n, send, device):
        ref = rowb.at[zz, rows_at(xx, n)]
        return remote(ref, ref, send, r_row.at[zz, xx, n], device)

    def up(zz, n):
        return row_copy(zz, x, n, s_up.at[zz, n], dev_z(z + 1))

    def down(zz, n):
        return row_copy(zz, x, n, s_dn.at[zz, n], dev_z(z - 1))

    def double(zz, n):
        return row_copy(zz, 1 - x, n, s_dup.at[jnp.where(zz == z, 0, 1), n], dev_z(inward))

    def across(zz, n):
        return row_copy(zz, x, n, s_x.at[zz, n], dev_x)

    def sideways(p, d, n):
        src = gb.at[0, gb_rows(c, n)] if p == 0 else rowb.at[ze, rows_at(x, n)]
        return remote(
            src, gb.at[p, gb_rows(c, n)], s_y.at[p, d, n], r_gb.at[p, c, n], dev_y(d)
        )

    def to_twin(d):
        cc = lax.rem(y + d, yn) * 2 + k
        ref = gb.at[0, gb_panel(cc)]
        return remote(ref, ref, s_c.at[0, d, 0], r_tw.at[0, cc, 0], dev_k)

    def edge_to_twin(d, n):
        cc = lax.rem(y + d, yn) * 2 + k
        dst = gb.at[1, gb_rows(cc, n)]
        src = rowb.at[ze, rows_at(x, n)] if d == 0 else dst
        return remote(src, dst, s_c.at[1, d, n], r_tw.at[1, cc, n], dev_k)

    def got_row(zz, xx, n):
        row_copy(zz, xx, n, s_dup.at[0, n], dev_x).wait_recv()

    def got_side(p, d, n):
        cc = lax.rem(y + d, yn) * 2 + k
        ref = gb.at[p, gb_rows(cc, n)]
        remote(ref, ref, s_dup.at[0, 0], r_gb.at[p, cc, n], dev_x).wait_recv()

    def got_twin(d):
        cc = lax.rem(y + d, yn) * 2 + 1 - k
        ref = gb.at[0, gb_panel(cc)]
        remote(ref, ref, s_dup.at[0, 0], r_tw.at[0, cc, 0], dev_x).wait_recv()

    def got_edge_twin(d):
        cc = lax.rem(y + d, yn) * 2 + 1 - k
        for n in range(CHUNKS):
            ref = gb.at[1, gb_rows(cc, n)]
            remote(ref, ref, s_dup.at[0, 0], r_tw.at[1, cc, n], dev_x).wait_recv()

    def own_sideways(chunks, do):
        for d in range(1, yn):
            for n in chunks:
                do(sideways(0, d, n))

    def x_own(n, do):
        if n < HALF:
            do(across(z, n))
        else:
            when(jnp.logical_not(proxy), lambda: do(across(z, n)))

    def z_own(n, do):
        when(z < zn - 1, lambda: do(up(z, n)))
        when(z > 0, lambda: do(down(z, n)))

    def own_sends(n, do):
        x_own(n, do)
        z_own(n, do)

    def y_arrivals(do, wait):
        for d in range(1, yn):
            if wait:
                for n in range(CHUNKS):
                    got_side(0, d, n)
            do(to_twin(d))

    def edge_arrivals(n, do, wait):
        for d in range(1, yn):
            if wait:
                got_side(1, d, n)
            do(edge_to_twin(d, n))

    def relay_z(zz, n, do):
        @pl.when(inside(zz) & (zz < z) & (z + 1 <= zn - 2))
        def _():
            do(up(zz, n))

        @pl.when(inside(zz) & (zz > z) & (z - 1 >= 1))
        def _():
            do(down(zz, n))

    def z_step(t, n):
        ahead = n + WINDOW
        dist, m = (t - 1, ahead) if ahead < CHUNKS else (t, ahead - CHUNKS)

        @pl.when(dist == 0)
        def _():
            x_own(m, start)
            z_own(m, start)

        @pl.when(dist != 0)
        def _():
            relay_z(z - dist, m, start)
            relay_z(z + dist, m, start)

    def relay(zz, n, do):
        dist = jnp.abs(zz - z)
        twice = ((zz == 0) | (zz == zn - 1)) & (
            (dist == 1) | ((dist == 2) & (n >= LAST))
        )

        @pl.when(jnp.logical_not(twice))
        def _():
            do(across(zz, n))

        adjacent = proxy & (zz == ze)

        @pl.when(adjacent)
        def _():
            for d in range(1, yn):
                do(sideways(1, d, n))
            do(edge_to_twin(0, n))

    def inside(zz):
        return (zz >= 0) & (zz <= zn - 1)

    def start(copy):
        copy.start()

    def finish(copy):
        copy.wait_send()

    step_rows = 2 * length

    def product(p, block, panel, store):
        at = pl.ds(pl.multiple_of(block * step_rows, step_rows), step_rows)
        store(at, lax.dot_general(
            gb[p, at, :], panel[...], (((1,), (1,)), ((), ())),
            preferred_element_type=jnp.float32,
        ).astype(ob.dtype))

    def slot_of(gg, q):
        return lax.rem(gg + half_span - q + rows_n, rows_n)

    def own_job(zz):
        slots = [slot_of(g, row_of(zz, xx)) for xx in range(2)]

        def store(at, value):
            for xx in range(2):
                ob[slots[xx], at, :] = value[:, xx * length:(xx + 1) * length]

        def body(i, carry):
            product(0, i, rowb.at[zz], store)
            return carry

        lax.fori_loop(0, yn, body, 0)

    def proxy_copy(q, block):
        s = slot_of(row_of(ze, x), q)
        at = pl.ds(pl.multiple_of(block * step_rows, step_rows), step_rows)
        return remote(
            pb.at[q, at], ob.at[s, at], s_p.at[q, block], r_ob.at[s, block], dev_z(ze)
        )

    def proxy_job(zz, xx, low_d, high_d):
        q = row_of(zz, xx)

        def store(at, value):
            pb[q, at, :] = value

        def body(d, carry):
            block = lax.rem(y + d, yn)
            panel = rowb.at[zz, pl.ds(pl.multiple_of(xx * length, length), length)]
            product(1, block, panel, store)
            proxy_copy(q, block).start()
            return carry

        lax.fori_loop(low_d, high_d, body, 0)

    neighbours = 2 + (yn - 1)
    pl.semaphore_wait(barrier, neighbours + jnp.where(edge, 1, 2))

    for n in range(WINDOW):
        own_sends(n, start)
    own_sideways(range(EARLY), start)
    to_twin(0).start()

    @pl.when(edge)
    def _():
        turned = [(m + HALF) % CHUNKS for m in range(CHUNKS)]
        own_sideways(range(EARLY, CHUNKS), start)
        for n in range(CHUNKS):
            got_row(z, 1 - x, n)
            got_row(inward, x, n)
            m = n + WINDOW
            if m < CHUNKS:
                own_sends(m, start)
            else:
                double(z, m - CHUNKS).start()
                across(inward, turned[m - CHUNKS]).start()
        y_arrivals(start, True)
        for n in range(CHUNKS):
            got_row(inward, 1 - x, turned[n])
            m = n + WINDOW
            if m < CHUNKS:
                double(z, m).start()
                across(inward, turned[m]).start()
            elif m - CHUNKS < CHUNKS - HALF:
                double(inward, turned[m - CHUNKS]).start()
        for d in range(yn):
            got_twin(d)

        def job(j, carry):
            own_job(jnp.where(j == 0, z, inward))
            return carry

        lax.fori_loop(0, 2, job, 0)

        for n in range(CHUNKS):
            own_sends(n, finish)
            double(z, n).wait_send()
            across(inward, n).wait_send()
            if n >= HALF:
                double(inward, n).wait_send()
        own_sideways(range(CHUNKS), finish)
        to_twin(0).wait_send()
        y_arrivals(finish, False)

        def far(i, carry):
            zz = inward + away * (i // 2 + 1)
            xx = jnp.where(lax.rem(i, 2) == 0, x, 1 - x)
            s = slot_of(g, row_of(zz, xx))
            for d in range(yn):
                block = lax.rem(y + d, yn)
                at = pl.ds(pl.multiple_of(block * step_rows, step_rows), step_rows)
                ref = ob.at[s, at]
                remote(ref, ref, s_p.at[0, 0], r_ob.at[s, block], dev_x).wait_recv()
            return carry

        lax.fori_loop(0, 2 * (zn - 2), far, 0)

    @pl.when(inner)
    def _():
        def settle():
            for n in range(CHUNKS):
                own_sends(n, finish)
            own_sideways(range(CHUNKS), finish)
            to_twin(0).wait_send()
            y_arrivals(finish, False)

            @pl.when(proxy)
            def _():
                for n in range(CHUNKS):
                    edge_arrivals(n, finish, False)
                for n in range(LAST, CHUNKS):
                    double(ze, n).wait_send()

            def relayed(zz, carry):
                @pl.when(zz != z)
                def _():
                    for n in range(CHUNKS):
                        relay(zz, n, finish)
                        relay_z(zz, n, finish)

                return carry

            lax.fori_loop(0, zn, relayed, 0)

        def turn(t, carry):
            first, second = t == 1, t == 2

            @pl.when(t == zn - 1)
            def _():
                settle()

            def forwards(n):
                for zz in (z - t * away, z + t * away):
                    @pl.when(inside(zz))
                    def _():
                        got_row(zz, x, n)
                        relay(zz, n, start)

                @pl.when(second & proxy)
                def _():
                    got_row(ze, 1 - x, n)
                    if n >= LAST:
                        double(ze, n).start()

            def proxied(dist, xx, low_d=0, high_d=yn):
                @pl.when(proxy & (dist >= 1) & inside(z + dist * away))
                def _():
                    proxy_job(z + dist * away, xx, low_d, high_d)

            def got_other(zz):
                @pl.when(inside(zz) & jnp.logical_not(proxy & (zz == ze)))
                def _():
                    for n in range(CHUNKS):
                        got_row(zz, 1 - x, n)

            for n in range(CHUNKS):
                if n == HALF:
                    @pl.when(t > 1)
                    def _():
                        got_other(z + (t - 1) * away)
                        proxied(t - 1, 1 - x)
                forwards(n)
                z_step(t, n)
                if n + EARLY < CHUNKS:
                    when(second, functools.partial(own_sideways, [n + EARLY], start))
                if n >= LAG:
                    @pl.when(first & proxy)
                    def _():
                        edge_arrivals(n - LAG, start, True)

            @pl.when(first & proxy)
            def _():
                gb[1, pl.ds(c0, length), :] = rowb[ze, pl.ds(x0, length), :]
                got_edge_twin(0)
                proxied(t, x, 0, 1)
                for n in range(CHUNKS - LAG, CHUNKS):
                    edge_arrivals(n, start, True)
                for d in range(1, yn):
                    got_edge_twin(d)
                proxied(t, x, 1)

            @pl.when(t > 1)
            def _():
                proxied(t, x)
                got_other(z - (t - 1) * away)

            @pl.when(second)
            def _():
                y_arrivals(start, True)
                for d in range(yn):
                    got_twin(d)

            def own(j, inner_carry):
                zz = z + jnp.where(j == 0, 1 - t, jnp.where(j == 1, t - 1, 0)) * away
                last = j == 2

                @pl.when(last & (t == zn - 1))
                def _():
                    for n in range(CHUNKS):
                        got_row(z, 1 - x, n)

                @pl.when(inside(zz) & (jnp.logical_not(last) | (t == zn - 1)))
                def _():
                    own_job(zz)

                return inner_carry

            @pl.when(t > 1)
            def _():
                lax.fori_loop(0, 3, own, 0)

            return carry

        lax.fori_loop(1, zn, turn, 0)

        @pl.when(proxy)
        def _():
            def sent(i, carry):
                zz = z + away * (i // 2 + 1)
                for d in range(yn):
                    proxy_copy(row_of(zz, lax.rem(i, 2)), d).wait_send()
                return carry

            lax.fori_loop(0, 2 * (zn - 2), sent, 0)


def local(density, pattern):
    rows_n, cols_n = lax.axis_size("row"), lax.axis_size("col")
    length, width = density.shape
    group = cols_n * length
    zn, yn = rows_n // 2, cols_n // 2
    kind = density.dtype
    dma = pltpu.SemaphoreType.DMA
    words = (2 * rows_n * group * length + (2 * group + rows_n * length + 2 * length) * width)
    out = pl.pallas_call(
        functools.partial(kernel, rows_n, cols_n),
        out_shape=jax.ShapeDtypeStruct((rows_n, group, length), kind),
        in_specs=[pl.BlockSpec(memory_space=pltpu.HBM)] * 2,
        out_specs=pl.BlockSpec(memory_space=pltpu.VMEM),
        scratch_shapes=[
            pltpu.VMEM((length, width), kind),
            pltpu.VMEM(pattern.shape, pattern.dtype),
            pltpu.VMEM((zn, 2 * length, width), kind),
            pltpu.VMEM((2, group, width), kind),
            pltpu.VMEM((rows_n, group, length), kind),
            dma((2,)),
            dma((zn, 2, CHUNKS)),
            dma((2, cols_n, CHUNKS)),
            dma((2, cols_n, CHUNKS)),
            dma((rows_n, yn)),
            dma((zn, CHUNKS)),
            dma((zn, CHUNKS)),
            dma((2, CHUNKS)),
            dma((zn, CHUNKS)),
            dma((2, yn, CHUNKS)),
            dma((2, yn, CHUNKS)),
            dma((rows_n, yn)),
        ],
        compiler_params=pltpu.CompilerParams(
            collective_id=0, has_side_effects=True, vmem_limit_bytes=2 * words + (8 << 20)
        ),
        cost_estimate=pl.CostEstimate(
            flops=2 * group * length * width * rows_n,
            bytes_accessed=2 * rows_n * group * length,
            transcendentals=0,
        ),
    )(*(pltpu.with_memory_space_constraint(a, pltpu.HBM) for a in (density, pattern)))
    return jnp.transpose(out, (1, 0, 2))


def solution(mesh):
    return jax.shard_map(
        local,
        mesh=mesh,
        in_specs=(P(("row", "col"), None), P(("row", "col"), None)),
        out_specs=P("row", None, "col"),
        check_vma=False,
    )
```

```python
import functools

import jax
import jax.numpy as jnp
from jax import lax
from jax.experimental import pallas as pl
from jax.experimental.pallas import tpu as pltpu
from jax.sharding import PartitionSpec as P

MESH = pl.DeviceIdType.MESH
CHUNKS = 4
HALF = CHUNKS // 2
EARLY = CHUNKS // 4
LAG = 2

def kernel(
    rows_n, cols_n, dens_hbm, pat_hbm, ob, dens, pat, rowb, gb, pb, s_in,
    r_row, r_gb, r_tw, r_ob, s_up, s_dn, s_dup, s_x, s_y, s_c, s_p,
):
    fetch_dens = pltpu.make_async_copy(dens_hbm, dens, s_in.at[0])
    fetch_pat = pltpu.make_async_copy(pat_hbm, pat, s_in.at[1])
    fetch_dens.start()
    fetch_pat.start()
    zn, yn = rows_n // 2, cols_n // 2
    length, width = dens.shape
    group = cols_n * length
    part = length // CHUNKS
    half_span = rows_n // 4
    g, c = lax.axis_index("row"), lax.axis_index("col")
    z, x = g // 2, lax.rem(g, 2)
    y, k = c // 2, lax.rem(c, 2)
    low, high = z == 0, z == zn - 1
    edge = low | high
    inner = jnp.logical_not(edge)
    proxy = (z == 1) | (z == zn - 2)
    away = jnp.where((z == 1) | low, 1, jnp.where((z == zn - 2) | high, -1, 1))
    inward = z + away
    ze = z - away

    def row_of(zz, xx):
        return zz * 2 + xx

    def when(cond, action):
        pl.when(cond)(action)

    def dev_z(zz):
        return (row_of(zz, x), c)

    dev_x = (row_of(z, 1 - x), c)
    dev_k = (g, y * 2 + 1 - k)

    def dev_y(d):
        return (g, lax.rem(y + d, yn) * 2 + k)

    barrier = pltpu.get_barrier_semaphore()

    def greet(device):
        pl.semaphore_signal(barrier, inc=1, device_id=device, device_id_type=MESH)

    greet(dev_x)
    greet(dev_k)
    for d in range(1, yn):
        greet(dev_y(d))
    when(z > 0, lambda: greet(dev_z(z - 1)))
    when(z < zn - 1, lambda: greet(dev_z(z + 1)))
    when(edge | (z == 2), lambda: greet(dev_z(jnp.where(edge, z + 2 * away, 0))))
    when(inner & (z == zn - 3), lambda: greet(dev_z(zn - 1)))

    def rows_at(xx, n):
        return pl.ds(pl.multiple_of(xx * length + n * part, part), part)

    def gb_rows(cc, n):
        return pl.ds(pl.multiple_of(cc * length + n * part, part), part)

    def gb_panel(cc):
        return pl.ds(pl.multiple_of(cc * length, length), length)

    blocks = pat.shape[0]
    size = length // blocks
    c0 = pl.multiple_of(c * length, length)
    x0 = pl.multiple_of(x * length, length)
    fetch_dens.wait()
    fetch_pat.wait()
    for b in range(blocks):
        for kb in range(pat.shape[1]):
            here = dens[b * size:(b + 1) * size, kb * size:(kb + 1) * size]
            keep = jnp.broadcast_to(pat[b:b + 1, kb:kb + 1], here.shape) != 0
            kept = jnp.where(keep, here.astype(jnp.float32), 0.0).astype(here.dtype)
            rowb[z, pl.ds(x0 + b * size, size), kb * size:(kb + 1) * size] = kept
            gb[0, pl.ds(c0 + b * size, size), kb * size:(kb + 1) * size] = kept

    def remote(src, dst, send, recv, device):
        return pltpu.make_async_remote_copy(
            src_ref=src, dst_ref=dst, send_sem=send, recv_sem=recv,
            device_id=device, device_id_type=MESH,
        )

    def row_copy(zz, xx, n, send, device):
        ref = rowb.at[zz, rows_at(xx, n)]
        return remote(ref, ref, send, r_row.at[zz, xx, n], device)

    def up(zz, n):
        return row_copy(zz, x, n, s_up.at[zz, n], dev_z(z + 1))

    def down(zz, n):
        return row_copy(zz, x, n, s_dn.at[zz, n], dev_z(z - 1))

    def double(n):
        return row_copy(z, 1 - x, n, s_dup.at[0, n], dev_z(inward))

    def direct(n):
        return row_copy(z, x, n, s_dup.at[1, n], dev_z(z + 2 * away))

    def across(zz, n):
        return row_copy(zz, x, n, s_x.at[zz, n], dev_x)

    def sideways(p, d, n):
        src = gb.at[0, gb_rows(c, n)] if p == 0 else rowb.at[ze, rows_at(x, n)]
        return remote(
            src, gb.at[p, gb_rows(c, n)], s_y.at[p, d, n], r_gb.at[p, c, n], dev_y(d)
        )

    def to_twin(d):
        cc = lax.rem(y + d, yn) * 2 + k
        ref = gb.at[0, gb_panel(cc)]
        return remote(ref, ref, s_c.at[0, d, 0], r_tw.at[0, cc, 0], dev_k)

    def edge_to_twin(d, n):
        cc = lax.rem(y + d, yn) * 2 + k
        dst = gb.at[1, gb_rows(cc, n)]
        src = rowb.at[ze, rows_at(x, n)] if d == 0 else dst
        return remote(src, dst, s_c.at[1, d, n], r_tw.at[1, cc, n], dev_k)

    def got_row(zz, xx, n):
        row_copy(zz, xx, n, s_dup.at[0, n], dev_x).wait_recv()

    def got_side(p, d, n):
        cc = lax.rem(y + d, yn) * 2 + k
        ref = gb.at[p, gb_rows(cc, n)]
        remote(ref, ref, s_dup.at[0, 0], r_gb.at[p, cc, n], dev_x).wait_recv()

    def got_twin(d):
        cc = lax.rem(y + d, yn) * 2 + 1 - k
        ref = gb.at[0, gb_panel(cc)]
        remote(ref, ref, s_dup.at[0, 0], r_tw.at[0, cc, 0], dev_x).wait_recv()

    def got_edge_twin(d):
        cc = lax.rem(y + d, yn) * 2 + 1 - k
        for n in range(CHUNKS):
            ref = gb.at[1, gb_rows(cc, n)]
            remote(ref, ref, s_dup.at[0, 0], r_tw.at[1, cc, n], dev_x).wait_recv()

    def own_sideways(chunks, do):
        for d in range(1, yn):
            for n in chunks:
                do(sideways(0, d, n))

    def own_sends(n, do):
        if n < HALF:
            do(across(z, n))
        else:
            when(jnp.logical_not(proxy), lambda: do(across(z, n)))
        when(z < zn - 1, lambda: do(up(z, n)))
        when(z > 0, lambda: do(down(z, n)))
        if n == CHUNKS - 1:
            do(to_twin(0))

    def late_sends(do):
        for n in range(HALF, CHUNKS):
            do(across(z, n))

    def y_arrivals(do, wait):
        for d in range(1, yn):
            if wait:
                for n in range(CHUNKS):
                    got_side(0, d, n)
            do(to_twin(d))

    def edge_arrivals(n, do, wait):
        for d in range(1, yn):
            if wait:
                got_side(1, d, n)
            do(edge_to_twin(d, n))

    def relay(zz, n, do):
        adjacent = proxy & (zz == ze)

        @pl.when((zz < z) & (z + 1 <= zn - 2) & jnp.logical_not(adjacent))
        def _():
            do(up(zz, n))

        @pl.when((zz > z) & (z - 1 >= 1) & jnp.logical_not(adjacent))
        def _():
            do(down(zz, n))

        @pl.when(jnp.logical_not(adjacent))
        def _():
            do(across(zz, n))

        @pl.when(adjacent)
        def _():
            for d in range(1, yn):
                do(sideways(1, d, n))
            do(edge_to_twin(0, n))

    def inside(zz):
        return (zz >= 0) & (zz <= zn - 1)

    def start(copy):
        copy.start()

    def finish(copy):
        copy.wait_send()

    step_rows = 2 * length

    def product(p, block, panel, store):
        at = pl.ds(pl.multiple_of(block * step_rows, step_rows), step_rows)
        store(at, lax.dot_general(
            gb[p, at, :], panel[...], (((1,), (1,)), ((), ())),
            preferred_element_type=jnp.float32,
        ).astype(ob.dtype))

    def slot_of(gg, q):
        return lax.rem(gg + half_span - q + rows_n, rows_n)

    def own_job(zz):
        slots = [slot_of(g, row_of(zz, xx)) for xx in range(2)]

        def store(at, value):
            for xx in range(2):
                ob[slots[xx], at, :] = value[:, xx * length:(xx + 1) * length]

        def body(i, carry):
            product(0, i, rowb.at[zz], store)
            return carry

        lax.fori_loop(0, yn, body, 0)

    def proxy_copy(q, block):
        s = slot_of(row_of(ze, x), q)
        at = pl.ds(pl.multiple_of(block * step_rows, step_rows), step_rows)
        return remote(
            pb.at[q, at], ob.at[s, at], s_p.at[q, block], r_ob.at[s, block], dev_z(ze)
        )

    def proxy_job(zz, xx, low_d, high_d):
        q = row_of(zz, xx)

        def store(at, value):
            pb[q, at, :] = value

        def body(d, carry):
            block = lax.rem(y + d, yn)
            panel = rowb.at[zz, pl.ds(pl.multiple_of(xx * length, length), length)]
            product(1, block, panel, store)
            proxy_copy(q, block).start()
            return carry

        lax.fori_loop(low_d, high_d, body, 0)

    neighbours = 2 + (yn - 1)
    pl.semaphore_wait(barrier, neighbours + jnp.where(
        edge, 2, 2 + jnp.where(z == 2, 1, 0) + jnp.where(z == zn - 3, 1, 0)
    ))

    for n in range(CHUNKS):
        own_sends(n, start)

        if n < EARLY:
            own_sideways([n], start)
        else:
            when(edge, functools.partial(own_sideways, [n], start))

    @pl.when(edge)
    def _():
        for n in range(CHUNKS):
            direct(n).start()
        for n in range(CHUNKS):
            got_row(z, 1 - x, n)
            double(n).start()
            got_row(inward, x, n)
            across(inward, n).start()
        y_arrivals(start, True)
        for d in range(yn):
            got_twin(d)

        def job(j, carry):
            @pl.when(j == 1)
            def _():
                for n in range(CHUNKS):
                    got_row(inward, 1 - x, n)

            own_job(jnp.where(j == 0, z, inward))
            return carry

        lax.fori_loop(0, 2, job, 0)

        for n in range(CHUNKS):
            own_sends(n, finish)
            double(n).wait_send()
            direct(n).wait_send()
            across(inward, n).wait_send()
        own_sideways(range(CHUNKS), finish)
        y_arrivals(finish, False)

        def far(i, carry):
            zz = inward + away * (i // 2 + 1)
            xx = jnp.where(lax.rem(i, 2) == 0, x, 1 - x)
            s = slot_of(g, row_of(zz, xx))
            for d in range(yn):
                block = lax.rem(y + d, yn)
                at = pl.ds(pl.multiple_of(block * step_rows, step_rows), step_rows)
                ref = ob.at[s, at]
                remote(ref, ref, s_p.at[0, 0], r_ob.at[s, block], dev_x).wait_recv()
            return carry

        lax.fori_loop(0, 2 * (zn - 2), far, 0)

    @pl.when(inner)
    def _():
        def settle():
            for n in range(CHUNKS):
                own_sends(n, finish)
            own_sideways(range(CHUNKS), finish)
            y_arrivals(finish, False)

            @pl.when(proxy)
            def _():
                for n in range(CHUNKS):
                    edge_arrivals(n, finish, False)
                late_sends(finish)

            def relayed(zz, carry):
                @pl.when(zz != z)
                def _():
                    for n in range(CHUNKS):
                        relay(zz, n, finish)

                return carry

            lax.fori_loop(0, zn, relayed, 0)

        def turn(t, carry):
            first, second = t == 1, t == 2

            @pl.when(t == zn - 1)
            def _():
                settle()

            def forwards(n):
                for zz in (z - t * away, z + t * away):
                    @pl.when(inside(zz))
                    def _():
                        got_row(zz, x, n)
                        relay(zz, n, start)

            def proxied(dist, xx, low_d=0, high_d=yn):
                @pl.when(proxy & (dist >= 1) & inside(z + dist * away))
                def _():
                    proxy_job(z + dist * away, xx, low_d, high_d)

            def got_other(zz):
                @pl.when(inside(zz) & jnp.logical_not(proxy & (zz == ze)))
                def _():
                    for n in range(CHUNKS):
                        got_row(zz, 1 - x, n)

            for n in range(CHUNKS):
                if n == HALF:
                    @pl.when(t > 1)
                    def _():
                        got_other(z + (t - 1) * away)
                        proxied(t - 1, 1 - x)
                forwards(n)
                if n >= LAG:
                    @pl.when(first & proxy)
                    def _():
                        edge_arrivals(n - LAG, start, True)

            @pl.when(first)
            def _():
                own_sideways(range(EARLY, CHUNKS), start)

            @pl.when(first & proxy)
            def _():
                gb[1, pl.ds(c0, length), :] = rowb[ze, pl.ds(x0, length), :]
                got_edge_twin(0)
                proxied(t, x, 0, 1)
                for n in range(CHUNKS - LAG, CHUNKS):
                    edge_arrivals(n, start, True)
                for d in range(1, yn):
                    got_edge_twin(d)
                proxied(t, x, 1)

            when(second & proxy, functools.partial(late_sends, start))

            @pl.when(t > 1)
            def _():
                proxied(t, x)
                got_other(z - (t - 1) * away)

            @pl.when(second)
            def _():
                y_arrivals(start, True)
                for d in range(yn):
                    got_twin(d)

            def own(j, inner_carry):
                zz = z + jnp.where(j == 0, 1 - t, jnp.where(j == 1, t - 1, 0)) * away
                zz = jnp.where(j == 3, ze, zz)
                late = j >= 2
                now = jnp.where(late, t == zn - 1, jnp.logical_not(proxy & (zz == ze)))
                now &= (j < 3) | proxy

                @pl.when(late & now)
                def _():
                    for n in range(CHUNKS):
                        got_row(zz, 1 - x, n)

                @pl.when(inside(zz) & now)
                def _():
                    own_job(zz)

                return inner_carry

            @pl.when(t > 1)
            def _():
                lax.fori_loop(0, 4, own, 0)

            return carry

        lax.fori_loop(1, zn, turn, 0)

        @pl.when(proxy)
        def _():
            def sent(i, carry):
                zz = z + away * (i // 2 + 1)
                for d in range(yn):
                    proxy_copy(row_of(zz, lax.rem(i, 2)), d).wait_send()
                return carry

            lax.fori_loop(0, 2 * (zn - 2), sent, 0)


def local(density, pattern):
    rows_n, cols_n = lax.axis_size("row"), lax.axis_size("col")
    length, width = density.shape
    group = cols_n * length
    zn, yn = rows_n // 2, cols_n // 2
    kind = density.dtype
    dma = pltpu.SemaphoreType.DMA
    words = (2 * rows_n * group * length + (2 * group + rows_n * length + 2 * length) * width)
    out = pl.pallas_call(
        functools.partial(kernel, rows_n, cols_n),
        out_shape=jax.ShapeDtypeStruct((rows_n, group, length), kind),
        in_specs=[pl.BlockSpec(memory_space=pltpu.HBM)] * 2,
        out_specs=pl.BlockSpec(memory_space=pltpu.VMEM),
        scratch_shapes=[
            pltpu.VMEM((length, width), kind),
            pltpu.VMEM(pattern.shape, pattern.dtype),
            pltpu.VMEM((zn, 2 * length, width), kind),
            pltpu.VMEM((2, group, width), kind),
            pltpu.VMEM((rows_n, group, length), kind),
            dma((2,)),
            dma((zn, 2, CHUNKS)),
            dma((2, cols_n, CHUNKS)),
            dma((2, cols_n, CHUNKS)),
            dma((rows_n, yn)),
            dma((zn, CHUNKS)),
            dma((zn, CHUNKS)),
            dma((2, CHUNKS)),
            dma((zn, CHUNKS)),
            dma((2, yn, CHUNKS)),
            dma((2, yn, CHUNKS)),
            dma((rows_n, yn)),
        ],
        compiler_params=pltpu.CompilerParams(
            collective_id=0, has_side_effects=True, vmem_limit_bytes=2 * words + (8 << 20)
        ),
        cost_estimate=pl.CostEstimate(
            flops=2 * group * length * width * rows_n,
            bytes_accessed=2 * rows_n * group * length,
            transcendentals=0,
        ),
    )(*(pltpu.with_memory_space_constraint(a, pltpu.HBM) for a in (density, pattern)))
    return jnp.transpose(out, (1, 0, 2))


def solution(mesh):
    return jax.shard_map(
        local,
        mesh=mesh,
        in_specs=(P(("row", "col"), None), P(("row", "col"), None)),
        out_specs=P("row", None, "col"),
        check_vma=False,
    )
```

```python
import functools

import jax
import jax.numpy as jnp
from jax import lax
from jax.experimental import pallas as pl
from jax.experimental.pallas import tpu as pltpu
from jax.sharding import PartitionSpec as P

MESH = pl.DeviceIdType.MESH
CHUNKS = 4
HALF = CHUNKS // 2
LAST = CHUNKS * 3 // 4
EARLY = CHUNKS // 2
LAG = 2

def kernel(
    rows_n, cols_n, dens_hbm, pat_hbm, ob, dens, pat, rowb, gb, pb, s_in,
    r_row, r_gb, r_tw, r_ob, s_up, s_dn, s_dup, s_x, s_y, s_c, s_p,
):
    fetch_dens = pltpu.make_async_copy(dens_hbm, dens, s_in.at[0])
    fetch_pat = pltpu.make_async_copy(pat_hbm, pat, s_in.at[1])
    fetch_dens.start()
    fetch_pat.start()
    zn, yn = rows_n // 2, cols_n // 2
    length, width = dens.shape
    group = cols_n * length
    part = length // CHUNKS
    half_span = rows_n // 4
    g, c = lax.axis_index("row"), lax.axis_index("col")
    z, x = g // 2, lax.rem(g, 2)
    y, k = c // 2, lax.rem(c, 2)
    low, high = z == 0, z == zn - 1
    edge = low | high
    inner = jnp.logical_not(edge)
    proxy = (z == 1) | (z == zn - 2)
    away = jnp.where((z == 1) | low, 1, jnp.where((z == zn - 2) | high, -1, 1))
    inward = z + away
    ze = z - away

    def row_of(zz, xx):
        return zz * 2 + xx

    def when(cond, action):
        pl.when(cond)(action)

    def dev_z(zz):
        return (row_of(zz, x), c)

    dev_x = (row_of(z, 1 - x), c)
    dev_k = (g, y * 2 + 1 - k)

    def dev_y(d):
        return (g, lax.rem(y + d, yn) * 2 + k)

    barrier = pltpu.get_barrier_semaphore()

    def greet(device):
        pl.semaphore_signal(barrier, inc=1, device_id=device, device_id_type=MESH)

    greet(dev_x)
    greet(dev_k)
    for d in range(1, yn):
        greet(dev_y(d))
    when(z > 0, lambda: greet(dev_z(z - 1)))
    when(z < zn - 1, lambda: greet(dev_z(z + 1)))

    def rows_at(xx, n):
        return pl.ds(pl.multiple_of(xx * length + n * part, part), part)

    def gb_rows(cc, n):
        return pl.ds(pl.multiple_of(cc * length + n * part, part), part)

    def gb_panel(cc):
        return pl.ds(pl.multiple_of(cc * length, length), length)

    blocks = pat.shape[0]
    size = length // blocks
    c0 = pl.multiple_of(c * length, length)
    x0 = pl.multiple_of(x * length, length)
    fetch_dens.wait()
    fetch_pat.wait()
    for b in range(blocks):
        for kb in range(pat.shape[1]):
            here = dens[b * size:(b + 1) * size, kb * size:(kb + 1) * size]
            keep = jnp.broadcast_to(pat[b:b + 1, kb:kb + 1], here.shape) != 0
            kept = jnp.where(keep, here.astype(jnp.float32), 0.0).astype(here.dtype)
            rowb[z, pl.ds(x0 + b * size, size), kb * size:(kb + 1) * size] = kept
            gb[0, pl.ds(c0 + b * size, size), kb * size:(kb + 1) * size] = kept

    def remote(src, dst, send, recv, device):
        return pltpu.make_async_remote_copy(
            src_ref=src, dst_ref=dst, send_sem=send, recv_sem=recv,
            device_id=device, device_id_type=MESH,
        )

    def row_copy(zz, xx, n, send, device):
        ref = rowb.at[zz, rows_at(xx, n)]
        return remote(ref, ref, send, r_row.at[zz, xx, n], device)

    def up(zz, n):
        return row_copy(zz, x, n, s_up.at[zz, n], dev_z(z + 1))

    def down(zz, n):
        return row_copy(zz, x, n, s_dn.at[zz, n], dev_z(z - 1))

    def double(zz, n):
        return row_copy(zz, 1 - x, n, s_dup.at[jnp.where(zz == z, 0, 1), n], dev_z(inward))

    def across(zz, n):
        return row_copy(zz, x, n, s_x.at[zz, n], dev_x)

    def sideways(p, d, n):
        src = gb.at[0, gb_rows(c, n)] if p == 0 else rowb.at[ze, rows_at(x, n)]
        return remote(
            src, gb.at[p, gb_rows(c, n)], s_y.at[p, d, n], r_gb.at[p, c, n], dev_y(d)
        )

    def to_twin(d):
        cc = lax.rem(y + d, yn) * 2 + k
        ref = gb.at[0, gb_panel(cc)]
        return remote(ref, ref, s_c.at[0, d, 0], r_tw.at[0, cc, 0], dev_k)

    def edge_to_twin(d, n):
        cc = lax.rem(y + d, yn) * 2 + k
        dst = gb.at[1, gb_rows(cc, n)]
        src = rowb.at[ze, rows_at(x, n)] if d == 0 else dst
        return remote(src, dst, s_c.at[1, d, n], r_tw.at[1, cc, n], dev_k)

    def got_row(zz, xx, n):
        row_copy(zz, xx, n, s_dup.at[0, n], dev_x).wait_recv()

    def got_side(p, d, n):
        cc = lax.rem(y + d, yn) * 2 + k
        ref = gb.at[p, gb_rows(cc, n)]
        remote(ref, ref, s_dup.at[0, 0], r_gb.at[p, cc, n], dev_x).wait_recv()

    def got_twin(d):
        cc = lax.rem(y + d, yn) * 2 + 1 - k
        ref = gb.at[0, gb_panel(cc)]
        remote(ref, ref, s_dup.at[0, 0], r_tw.at[0, cc, 0], dev_x).wait_recv()

    def got_edge_twin(d):
        cc = lax.rem(y + d, yn) * 2 + 1 - k
        for n in range(CHUNKS):
            ref = gb.at[1, gb_rows(cc, n)]
            remote(ref, ref, s_dup.at[0, 0], r_tw.at[1, cc, n], dev_x).wait_recv()

    def own_sideways(chunks, do):
        for d in range(1, yn):
            for n in chunks:
                do(sideways(0, d, n))

    def own_sends(n, do):
        if n < HALF:
            do(across(z, n))
        else:
            when(jnp.logical_not(proxy), lambda: do(across(z, n)))
        when(z < zn - 1, lambda: do(up(z, n)))
        when(z > 0, lambda: do(down(z, n)))
        if n == CHUNKS - 1:
            do(to_twin(0))

    def y_arrivals(do, wait):
        for d in range(1, yn):
            if wait:
                for n in range(CHUNKS):
                    got_side(0, d, n)
            do(to_twin(d))

    def edge_arrivals(n, do, wait):
        for d in range(1, yn):
            if wait:
                got_side(1, d, n)
            do(edge_to_twin(d, n))

    def relay(zz, n, do):
        @pl.when((zz < z) & (z + 1 <= zn - 2))
        def _():
            do(up(zz, n))

        @pl.when((zz > z) & (z - 1 >= 1))
        def _():
            do(down(zz, n))

        dist = jnp.abs(zz - z)
        twice = ((zz == 0) | (zz == zn - 1)) & (
            (dist == 1) | ((dist == 2) & (n >= LAST))
        )

        @pl.when(jnp.logical_not(twice))
        def _():
            do(across(zz, n))

        adjacent = proxy & (zz == ze)

        @pl.when(adjacent)
        def _():
            for d in range(1, yn):
                do(sideways(1, d, n))
            do(edge_to_twin(0, n))

    def inside(zz):
        return (zz >= 0) & (zz <= zn - 1)

    def start(copy):
        copy.start()

    def finish(copy):
        copy.wait_send()

    step_rows = 2 * length

    def product(p, block, panel, store):
        at = pl.ds(pl.multiple_of(block * step_rows, step_rows), step_rows)
        store(at, lax.dot_general(
            gb[p, at, :], panel[...], (((1,), (1,)), ((), ())),
            preferred_element_type=jnp.float32,
        ).astype(ob.dtype))

    def slot_of(gg, q):
        return lax.rem(gg + half_span - q + rows_n, rows_n)

    def own_job(zz):
        slots = [slot_of(g, row_of(zz, xx)) for xx in range(2)]

        def store(at, value):
            for xx in range(2):
                ob[slots[xx], at, :] = value[:, xx * length:(xx + 1) * length]

        def body(i, carry):
            product(0, i, rowb.at[zz], store)
            return carry

        lax.fori_loop(0, yn, body, 0)

    def proxy_copy(q, block):
        s = slot_of(row_of(ze, x), q)
        at = pl.ds(pl.multiple_of(block * step_rows, step_rows), step_rows)
        return remote(
            pb.at[q, at], ob.at[s, at], s_p.at[q, block], r_ob.at[s, block], dev_z(ze)
        )

    def proxy_job(zz, xx, low_d, high_d):
        q = row_of(zz, xx)

        def store(at, value):
            pb[q, at, :] = value

        def body(d, carry):
            block = lax.rem(y + d, yn)
            panel = rowb.at[zz, pl.ds(pl.multiple_of(xx * length, length), length)]
            product(1, block, panel, store)
            proxy_copy(q, block).start()
            return carry

        lax.fori_loop(low_d, high_d, body, 0)

    neighbours = 2 + (yn - 1)
    pl.semaphore_wait(barrier, neighbours + jnp.where(edge, 1, 2))

    for n in range(CHUNKS):
        own_sends(n, start)

        if n < EARLY:
            own_sideways([n], start)
        else:
            when(edge, functools.partial(own_sideways, [n], start))

    @pl.when(edge)
    def _():
        for n in range(CHUNKS):
            got_row(z, 1 - x, n)
            double(z, n).start()
            got_row(inward, x, n)
            across(inward, n).start()
        y_arrivals(start, True)
        for d in range(yn):
            got_twin(d)

        def job(j, carry):
            @pl.when(j == 1)
            def _():
                for n in range(CHUNKS):
                    got_row(inward, 1 - x, n)
                    if n >= HALF:
                        double(inward, n).start()

            own_job(jnp.where(j == 0, z, inward))
            return carry

        lax.fori_loop(0, 2, job, 0)

        for n in range(CHUNKS):
            own_sends(n, finish)
            double(z, n).wait_send()
            across(inward, n).wait_send()
            if n >= HALF:
                double(inward, n).wait_send()
        own_sideways(range(CHUNKS), finish)
        y_arrivals(finish, False)

        def far(i, carry):
            zz = inward + away * (i // 2 + 1)
            xx = jnp.where(lax.rem(i, 2) == 0, x, 1 - x)
            s = slot_of(g, row_of(zz, xx))
            for d in range(yn):
                block = lax.rem(y + d, yn)
                at = pl.ds(pl.multiple_of(block * step_rows, step_rows), step_rows)
                ref = ob.at[s, at]
                remote(ref, ref, s_p.at[0, 0], r_ob.at[s, block], dev_x).wait_recv()
            return carry

        lax.fori_loop(0, 2 * (zn - 2), far, 0)

    @pl.when(inner)
    def _():
        def settle():
            for n in range(CHUNKS):
                own_sends(n, finish)
            own_sideways(range(CHUNKS), finish)
            y_arrivals(finish, False)

            @pl.when(proxy)
            def _():
                for n in range(CHUNKS):
                    edge_arrivals(n, finish, False)
                for n in range(LAST, CHUNKS):
                    double(ze, n).wait_send()

            def relayed(zz, carry):
                @pl.when(zz != z)
                def _():
                    for n in range(CHUNKS):
                        relay(zz, n, finish)

                return carry

            lax.fori_loop(0, zn, relayed, 0)

        def turn(t, carry):
            first, second = t == 1, t == 2

            @pl.when(t == zn - 1)
            def _():
                settle()

            def forwards(n):
                for zz in (z - t * away, z + t * away):
                    @pl.when(inside(zz))
                    def _():
                        got_row(zz, x, n)
                        relay(zz, n, start)

                @pl.when(second & proxy)
                def _():
                    got_row(ze, 1 - x, n)
                    if n >= LAST:
                        double(ze, n).start()

            def proxied(dist, xx, low_d=0, high_d=yn):
                @pl.when(proxy & (dist >= 1) & inside(z + dist * away))
                def _():
                    proxy_job(z + dist * away, xx, low_d, high_d)

            def got_other(zz):
                @pl.when(inside(zz) & jnp.logical_not(proxy & (zz == ze)))
                def _():
                    for n in range(CHUNKS):
                        got_row(zz, 1 - x, n)

            for n in range(CHUNKS):
                if n == HALF:
                    @pl.when(t > 1)
                    def _():
                        got_other(z + (t - 1) * away)
                        proxied(t - 1, 1 - x)
                forwards(n)
                if n >= LAG:
                    @pl.when(first & proxy)
                    def _():
                        edge_arrivals(n - LAG, start, True)

            @pl.when(first)
            def _():
                own_sideways(range(EARLY, CHUNKS), start)

            @pl.when(first & proxy)
            def _():
                gb[1, pl.ds(c0, length), :] = rowb[ze, pl.ds(x0, length), :]
                got_edge_twin(0)
                proxied(t, x, 0, 1)
                for n in range(CHUNKS - LAG, CHUNKS):
                    edge_arrivals(n, start, True)
                for d in range(1, yn):
                    got_edge_twin(d)
                proxied(t, x, 1)

            @pl.when(t > 1)
            def _():
                proxied(t, x)
                got_other(z - (t - 1) * away)

            when(second, functools.partial(y_arrivals, start, True))

            @pl.when(t == 3)
            def _():
                for d in range(yn):
                    got_twin(d)

            def own(j, inner_carry):
                dist = jnp.where(j < 2, t - 2, jnp.where(j < 4, t - 1, 0))
                zz = z + jnp.where(lax.rem(j, 2) == 0, dist, -dist) * away
                last = t == zn - 1

                @pl.when((j == 4) & last)
                def _():
                    for n in range(CHUNKS):
                        got_row(z, 1 - x, n)

                @pl.when(inside(zz) & ((j < 2) | last))
                def _():
                    own_job(zz)

                return inner_carry

            @pl.when(t > 2)
            def _():
                lax.fori_loop(0, 5, own, 0)

            return carry

        lax.fori_loop(1, zn, turn, 0)

        @pl.when(proxy)
        def _():
            def sent(i, carry):
                zz = z + away * (i // 2 + 1)
                for d in range(yn):
                    proxy_copy(row_of(zz, lax.rem(i, 2)), d).wait_send()
                return carry

            lax.fori_loop(0, 2 * (zn - 2), sent, 0)


def local(density, pattern):
    rows_n, cols_n = lax.axis_size("row"), lax.axis_size("col")
    length, width = density.shape
    group = cols_n * length
    zn, yn = rows_n // 2, cols_n // 2
    kind = density.dtype
    dma = pltpu.SemaphoreType.DMA
    words = (2 * rows_n * group * length + (2 * group + rows_n * length + 2 * length) * width)
    out = pl.pallas_call(
        functools.partial(kernel, rows_n, cols_n),
        out_shape=jax.ShapeDtypeStruct((rows_n, group, length), kind),
        in_specs=[pl.BlockSpec(memory_space=pltpu.HBM)] * 2,
        out_specs=pl.BlockSpec(memory_space=pltpu.VMEM),
        scratch_shapes=[
            pltpu.VMEM((length, width), kind),
            pltpu.VMEM(pattern.shape, pattern.dtype),
            pltpu.VMEM((zn, 2 * length, width), kind),
            pltpu.VMEM((2, group, width), kind),
            pltpu.VMEM((rows_n, group, length), kind),
            dma((2,)),
            dma((zn, 2, CHUNKS)),
            dma((2, cols_n, CHUNKS)),
            dma((2, cols_n, CHUNKS)),
            dma((rows_n, yn)),
            dma((zn, CHUNKS)),
            dma((zn, CHUNKS)),
            dma((2, CHUNKS)),
            dma((zn, CHUNKS)),
            dma((2, yn, CHUNKS)),
            dma((2, yn, CHUNKS)),
            dma((rows_n, yn)),
        ],
        compiler_params=pltpu.CompilerParams(
            collective_id=0, has_side_effects=True, vmem_limit_bytes=2 * words + (8 << 20)
        ),
        cost_estimate=pl.CostEstimate(
            flops=2 * group * length * width * rows_n,
            bytes_accessed=2 * rows_n * group * length,
            transcendentals=0,
        ),
    )(*(pltpu.with_memory_space_constraint(a, pltpu.HBM) for a in (density, pattern)))
    return jnp.transpose(out, (1, 0, 2))


def solution(mesh):
    return jax.shard_map(
        local,
        mesh=mesh,
        in_specs=(P(("row", "col"), None), P(("row", "col"), None)),
        out_specs=P("row", None, "col"),
        check_vma=False,
    )
```

```python
import functools

import jax
import jax.numpy as jnp
from jax import lax
from jax.experimental import pallas as pl
from jax.experimental.pallas import tpu as pltpu
from jax.sharding import PartitionSpec as P

MESH = pl.DeviceIdType.MESH
CHUNKS = 2
HALF = CHUNKS // 2
LAST = CHUNKS - 1


def kernel(
    rows_n, cols_n, dens_hbm, pat_hbm, ob, dens, pat, rowb, gb, pb, s_in,
    r_row, r_gb, r_tw, r_ob, s_up, s_dn, s_dup, s_x, s_y, s_c, s_p,
):
    fetch_dens = pltpu.make_async_copy(dens_hbm, dens, s_in.at[0])
    fetch_pat = pltpu.make_async_copy(pat_hbm, pat, s_in.at[1])
    fetch_dens.start()
    fetch_pat.start()
    zn, yn = rows_n // 2, cols_n // 2
    length, width = dens.shape
    group = cols_n * length
    part = length // CHUNKS
    half_span = rows_n // 4
    g, c = lax.axis_index("row"), lax.axis_index("col")
    z, x = g // 2, lax.rem(g, 2)
    y, k = c // 2, lax.rem(c, 2)
    low, high = z == 0, z == zn - 1
    edge = low | high
    inner = jnp.logical_not(edge)
    proxy = (z == 1) | (z == zn - 2)
    away = jnp.where((z == 1) | low, 1, jnp.where((z == zn - 2) | high, -1, 1))
    inward = z + away
    ze = z - away

    def row_of(zz, xx):
        return zz * 2 + xx

    def when(cond, action):
        pl.when(cond)(action)

    def dev_z(zz):
        return (row_of(zz, x), c)

    dev_x = (row_of(z, 1 - x), c)
    dev_k = (g, y * 2 + 1 - k)

    def dev_y(d):
        return (g, lax.rem(y + d, yn) * 2 + k)

    barrier = pltpu.get_barrier_semaphore()

    def greet(device):
        pl.semaphore_signal(barrier, inc=1, device_id=device, device_id_type=MESH)

    greet(dev_x)
    greet(dev_k)
    for d in range(1, yn):
        greet(dev_y(d))
    when(z > 0, lambda: greet(dev_z(z - 1)))
    when(z < zn - 1, lambda: greet(dev_z(z + 1)))

    def rows_at(xx, n):
        return pl.ds(pl.multiple_of(xx * length + n * part, part), part)

    side = length // 2

    def gb_half(cc, h):
        return pl.ds(pl.multiple_of(cc * length + h * side, side), side)

    def gb_panel(cc):
        return pl.ds(pl.multiple_of(cc * length, length), length)

    blocks = pat.shape[0]
    size = length // blocks
    c0 = pl.multiple_of(c * length, length)
    x0 = pl.multiple_of(x * length, length)
    fetch_dens.wait()
    fetch_pat.wait()
    for b in range(blocks):
        for kb in range(pat.shape[1]):
            here = dens[b * size:(b + 1) * size, kb * size:(kb + 1) * size]
            keep = jnp.broadcast_to(pat[b:b + 1, kb:kb + 1], here.shape) != 0
            kept = jnp.where(keep, here.astype(jnp.float32), 0.0).astype(here.dtype)
            rowb[z, pl.ds(x0 + b * size, size), kb * size:(kb + 1) * size] = kept
            gb[0, pl.ds(c0 + b * size, size), kb * size:(kb + 1) * size] = kept

    def remote(src, dst, send, recv, device):
        return pltpu.make_async_remote_copy(
            src_ref=src, dst_ref=dst, send_sem=send, recv_sem=recv,
            device_id=device, device_id_type=MESH,
        )

    def row_copy(zz, xx, n, send, device):
        ref = rowb.at[zz, rows_at(xx, n)]
        return remote(ref, ref, send, r_row.at[zz, xx, n], device)

    def up(zz, n):
        return row_copy(zz, x, n, s_up.at[zz, n], dev_z(z + 1))

    def down(zz, n):
        return row_copy(zz, x, n, s_dn.at[zz, n], dev_z(z - 1))

    def double(zz, n):
        return row_copy(zz, 1 - x, n, s_dup.at[jnp.where(zz == z, 0, 1), n], dev_z(inward))

    def across(zz, n):
        return row_copy(zz, x, n, s_x.at[zz, n], dev_x)

    def sideways(p, d, h):
        if p == 0:
            src = gb.at[0, gb_half(c, h)]
        else:
            src = rowb.at[ze, pl.ds(pl.multiple_of(x * length + h * side, side), side)]
        return remote(
            src, gb.at[p, gb_half(c, h)], s_y.at[p, d, h], r_gb.at[p, c, h], dev_y(d)
        )

    def to_twin(p, d):
        cc = lax.rem(y + d, yn) * 2 + k
        if p == 1 and d == 0:
            src = rowb.at[ze, pl.ds(x0, length)]
        else:
            src = gb.at[p, gb_panel(cc)]
        return remote(src, gb.at[p, gb_panel(cc)], s_c.at[p, d], r_tw.at[p, cc], dev_k)

    def got_row(zz, xx, n):
        row_copy(zz, xx, n, s_dup.at[0, n], dev_x).wait_recv()

    def got_side(p, d, h):
        cc = lax.rem(y + d, yn) * 2 + k
        ref = gb.at[p, gb_half(cc, h)]
        remote(ref, ref, s_dup.at[0, 0], r_gb.at[p, cc, h], dev_x).wait_recv()

    def got_twin(p, d):
        cc = lax.rem(y + d, yn) * 2 + 1 - k
        ref = gb.at[p, gb_panel(cc)]
        remote(ref, ref, s_dup.at[0, 0], r_tw.at[p, cc], dev_x).wait_recv()

    def own_sideways(h, do):
        for d in range(1, yn):
            do(sideways(0, d, h))

    def own_sends(n, do):
        if n < HALF:
            do(across(z, n))
        else:
            when(jnp.logical_not(proxy), lambda: do(across(z, n)))
        when(z < zn - 1, lambda: do(up(z, n)))
        when(z > 0, lambda: do(down(z, n)))
        if n == CHUNKS - 1:
            do(to_twin(0, 0))

    def y_arrivals(p, do, wait):
        for d in range(1, yn):
            if wait:
                for h in range(2):
                    got_side(p, d, h)
            do(to_twin(p, d))

    def relay(zz, n, do):
        @pl.when((zz < z) & (z + 1 <= zn - 2))
        def _():
            do(up(zz, n))

        @pl.when((zz > z) & (z - 1 >= 1))
        def _():
            do(down(zz, n))

        dist = jnp.abs(zz - z)
        twice = ((zz == 0) | (zz == zn - 1)) & (
            (dist == 1) | ((dist == 2) & (n >= LAST))
        )

        @pl.when(jnp.logical_not(twice))
        def _():
            do(across(zz, n))

        adjacent = proxy & (zz == ze)

        @pl.when(adjacent)
        def _():
            if n % HALF == HALF - 1:
                for d in range(1, yn):
                    do(sideways(1, d, n // HALF))
            if n == CHUNKS - 1:
                do(to_twin(1, 0))

    def inside(zz):
        return (zz >= 0) & (zz <= zn - 1)

    def start(copy):
        copy.start()

    def finish(copy):
        copy.wait_send()

    step_rows = 2 * length

    def product(p, block, panel, store):
        at = pl.ds(pl.multiple_of(block * step_rows, step_rows), step_rows)
        store(at, lax.dot_general(
            gb[p, at, :], panel[...], (((1,), (1,)), ((), ())),
            preferred_element_type=jnp.float32,
        ).astype(ob.dtype))

    def slot_of(gg, q):
        return lax.rem(gg + half_span - q + rows_n, rows_n)

    def own_job(zz):
        slots = [slot_of(g, row_of(zz, xx)) for xx in range(2)]

        def store(at, value):
            for xx in range(2):
                ob[slots[xx], at, :] = value[:, xx * length:(xx + 1) * length]

        def body(i, carry):
            product(0, i, rowb.at[zz], store)
            return carry

        lax.fori_loop(0, yn, body, 0)

    def proxy_copy(q, block):
        s = slot_of(row_of(ze, x), q)
        at = pl.ds(pl.multiple_of(block * step_rows, step_rows), step_rows)
        return remote(
            pb.at[q, at], ob.at[s, at], s_p.at[q, block], r_ob.at[s, block], dev_z(ze)
        )

    def proxy_job(zz, xx, low_d, high_d):
        q = row_of(zz, xx)

        def store(at, value):
            pb[q, at, :] = value

        def body(d, carry):
            block = lax.rem(y + d, yn)
            panel = rowb.at[zz, pl.ds(pl.multiple_of(xx * length, length), length)]
            product(1, block, panel, store)
            proxy_copy(q, block).start()
            return carry

        lax.fori_loop(low_d, high_d, body, 0)

    neighbours = 2 + (yn - 1)
    pl.semaphore_wait(barrier, neighbours + jnp.where(edge, 1, 2))

    for n in range(CHUNKS):
        own_sends(n, start)

        if n == HALF - 1:
            own_sideways(0, start)
        if n == CHUNKS - 1:
            when(edge, lambda: own_sideways(1, start))

    @pl.when(edge)
    def _():
        for n in range(CHUNKS):
            got_row(z, 1 - x, n)
            double(z, n).start()
            got_row(inward, x, n)
            across(inward, n).start()
        y_arrivals(0, start, True)
        for d in range(yn):
            got_twin(0, d)

        def job(j, carry):
            @pl.when(j == 1)
            def _():
                for n in range(CHUNKS):
                    got_row(inward, 1 - x, n)
                    if n >= HALF:
                        double(inward, n).start()

            own_job(jnp.where(j == 0, z, inward))
            return carry

        lax.fori_loop(0, 2, job, 0)

        for n in range(CHUNKS):
            own_sends(n, finish)
            double(z, n).wait_send()
            across(inward, n).wait_send()
            if n >= HALF:
                double(inward, n).wait_send()
        own_sideways(0, finish)
        own_sideways(1, finish)
        y_arrivals(0, finish, False)

        def far(i, carry):
            zz = inward + away * (i // 2 + 1)
            xx = jnp.where(lax.rem(i, 2) == 0, x, 1 - x)
            s = slot_of(g, row_of(zz, xx))
            for d in range(yn):
                block = lax.rem(y + d, yn)
                at = pl.ds(pl.multiple_of(block * step_rows, step_rows), step_rows)
                ref = ob.at[s, at]
                remote(ref, ref, s_p.at[0, 0], r_ob.at[s, block], dev_x).wait_recv()
            return carry

        lax.fori_loop(0, 2 * (zn - 2), far, 0)

    @pl.when(inner)
    def _():
        def settle():
            for n in range(CHUNKS):
                own_sends(n, finish)
            own_sideways(0, finish)
            own_sideways(1, finish)
            y_arrivals(0, finish, False)

            @pl.when(proxy)
            def _():
                y_arrivals(1, finish, False)
                for n in range(LAST, CHUNKS):
                    double(ze, n).wait_send()

            def relayed(zz, carry):
                @pl.when(zz != z)
                def _():
                    for n in range(CHUNKS):
                        relay(zz, n, finish)

                return carry

            lax.fori_loop(0, zn, relayed, 0)

        def turn(t, carry):
            first, second = t == 1, t == 2

            @pl.when(t == zn - 1)
            def _():
                settle()


            def forwards(n):
                for zz in (z - t * away, z + t * away):
                    @pl.when(inside(zz))
                    def _():
                        got_row(zz, x, n)
                        relay(zz, n, start)

                @pl.when(second & proxy)
                def _():
                    got_row(ze, 1 - x, n)
                    if n >= LAST:
                        double(ze, n).start()

            def proxied(dist, xx, low_d=0, high_d=yn):
                @pl.when(proxy & (dist >= 1) & inside(z + dist * away))
                def _():
                    proxy_job(z + dist * away, xx, low_d, high_d)

            def got_other(zz):
                @pl.when(inside(zz) & jnp.logical_not(proxy & (zz == ze)))
                def _():
                    for n in range(CHUNKS):
                        got_row(zz, 1 - x, n)

            for n in range(HALF):
                forwards(n)

            @pl.when(second & proxy)
            def _():
                y_arrivals(1, start, True)
                for d in range(1, yn):
                    got_twin(1, d)
                proxied(t - 1, x, 1)

            for n in range(HALF, CHUNKS):
                if n == LAST:
                    @pl.when(t > 1)
                    def _():
                        got_other(z + (t - 1) * away)
                        proxied(t - 1, 1 - x)
                forwards(n)

            @pl.when(first)
            def _():
                own_sideways(1, start)

            @pl.when(first & proxy)
            def _():
                gb[1, pl.ds(c0, length), :] = rowb[ze, pl.ds(x0, length), :]
                got_twin(1, 0)
                proxied(t, x, 0, 1)

            @pl.when(t > 1)
            def _():
                proxied(t, x)
                got_other(z - (t - 1) * away)

            @pl.when(second)
            def _():
                y_arrivals(0, start, True)
                for d in range(yn):
                    got_twin(0, d)

            def own(j, inner_carry):
                zz = z + jnp.where(j == 0, 1 - t, jnp.where(j == 1, t - 1, 0)) * away
                last = j == 2

                @pl.when(last & (t == zn - 1))
                def _():
                    for n in range(CHUNKS):
                        got_row(z, 1 - x, n)

                @pl.when(inside(zz) & (jnp.logical_not(last) | (t == zn - 1)))
                def _():
                    own_job(zz)

                return inner_carry

            @pl.when(t > 1)
            def _():
                lax.fori_loop(0, 3, own, 0)

            return carry

        lax.fori_loop(1, zn, turn, 0)

        @pl.when(proxy)
        def _():
            def sent(i, carry):
                zz = z + away * (i // 2 + 1)
                for d in range(yn):
                    proxy_copy(row_of(zz, lax.rem(i, 2)), d).wait_send()
                return carry

            lax.fori_loop(0, 2 * (zn - 2), sent, 0)


def local(density, pattern):
    rows_n, cols_n = lax.axis_size("row"), lax.axis_size("col")
    length, width = density.shape
    group = cols_n * length
    zn, yn = rows_n // 2, cols_n // 2
    kind = density.dtype
    dma = pltpu.SemaphoreType.DMA
    words = (2 * rows_n * group * length + (2 * group + rows_n * length + 2 * length) * width)
    out = pl.pallas_call(
        functools.partial(kernel, rows_n, cols_n),
        out_shape=jax.ShapeDtypeStruct((rows_n, group, length), kind),
        in_specs=[pl.BlockSpec(memory_space=pltpu.HBM)] * 2,
        out_specs=pl.BlockSpec(memory_space=pltpu.VMEM),
        scratch_shapes=[
            pltpu.VMEM((length, width), kind),
            pltpu.VMEM(pattern.shape, pattern.dtype),
            pltpu.VMEM((zn, 2 * length, width), kind),
            pltpu.VMEM((2, group, width), kind),
            pltpu.VMEM((rows_n, group, length), kind),
            dma((2,)),
            dma((zn, 2, CHUNKS)),
            dma((2, cols_n, 2)),
            dma((2, cols_n)),
            dma((rows_n, yn)),
            dma((zn, CHUNKS)),
            dma((zn, CHUNKS)),
            dma((2, CHUNKS)),
            dma((zn, CHUNKS)),
            dma((2, yn, 2)),
            dma((2, yn)),
            dma((rows_n, yn)),
        ],
        compiler_params=pltpu.CompilerParams(
            collective_id=0, has_side_effects=True, vmem_limit_bytes=2 * words + (8 << 20)
        ),
        cost_estimate=pl.CostEstimate(
            flops=2 * group * length * width * rows_n,
            bytes_accessed=2 * rows_n * group * length,
            transcendentals=0,
        ),
    )(*(pltpu.with_memory_space_constraint(a, pltpu.HBM) for a in (density, pattern)))
    return jnp.transpose(out, (1, 0, 2))


def solution(mesh):
    return jax.shard_map(
        local,
        mesh=mesh,
        in_specs=(P(("row", "col"), None), P(("row", "col"), None)),
        out_specs=P("row", None, "col"),
        check_vma=False,
    )
```

```python
import functools

import jax
import jax.numpy as jnp
from jax import lax
from jax.experimental import pallas as pl
from jax.experimental.pallas import tpu as pltpu
from jax.sharding import PartitionSpec as P

MESH = pl.DeviceIdType.MESH
CHUNKS = 4
HALF = CHUNKS // 2
LAST = CHUNKS


def kernel(
    rows_n, cols_n, dens_hbm, pat_hbm, ob, dens, pat, rowb, gb, pb, s_in,
    r_row, r_gb, r_tw, r_ob, s_up, s_dn, s_dup, s_x, s_y, s_c, s_p,
):
    fetch_dens = pltpu.make_async_copy(dens_hbm, dens, s_in.at[0])
    fetch_pat = pltpu.make_async_copy(pat_hbm, pat, s_in.at[1])
    fetch_dens.start()
    fetch_pat.start()
    zn, yn = rows_n // 2, cols_n // 2
    length, width = dens.shape
    group = cols_n * length
    part = length // CHUNKS
    half_span = rows_n // 4
    g, c = lax.axis_index("row"), lax.axis_index("col")
    z, x = g // 2, lax.rem(g, 2)
    y, k = c // 2, lax.rem(c, 2)
    low, high = z == 0, z == zn - 1
    edge = low | high
    inner = jnp.logical_not(edge)
    proxy = (z == 1) | (z == zn - 2)
    away = jnp.where((z == 1) | low, 1, jnp.where((z == zn - 2) | high, -1, 1))
    inward = z + away
    ze = z - away

    def row_of(zz, xx):
        return zz * 2 + xx

    def when(cond, action):
        pl.when(cond)(action)

    def dev_z(zz):
        return (row_of(zz, x), c)

    dev_x = (row_of(z, 1 - x), c)
    dev_k = (g, y * 2 + 1 - k)

    def dev_y(d):
        return (g, lax.rem(y + d, yn) * 2 + k)

    barrier = pltpu.get_barrier_semaphore()

    def greet(device):
        pl.semaphore_signal(barrier, inc=1, device_id=device, device_id_type=MESH)

    greet(dev_x)
    greet(dev_k)
    for d in range(1, yn):
        greet(dev_y(d))
    when(z > 0, lambda: greet(dev_z(z - 1)))
    when(z < zn - 1, lambda: greet(dev_z(z + 1)))

    def rows_at(xx, n):
        return pl.ds(pl.multiple_of(xx * length + n * part, part), part)

    side = length // 2

    def gb_half(cc, h):
        return pl.ds(pl.multiple_of(cc * length + h * side, side), side)

    def gb_panel(cc):
        return pl.ds(pl.multiple_of(cc * length, length), length)

    blocks = pat.shape[0]
    size = length // blocks
    c0 = pl.multiple_of(c * length, length)
    x0 = pl.multiple_of(x * length, length)
    fetch_dens.wait()
    fetch_pat.wait()
    for b in range(blocks):
        for kb in range(pat.shape[1]):
            here = dens[b * size:(b + 1) * size, kb * size:(kb + 1) * size]
            keep = jnp.broadcast_to(pat[b:b + 1, kb:kb + 1], here.shape) != 0
            kept = jnp.where(keep, here.astype(jnp.float32), 0.0).astype(here.dtype)
            rowb[z, pl.ds(x0 + b * size, size), kb * size:(kb + 1) * size] = kept
            gb[0, pl.ds(c0 + b * size, size), kb * size:(kb + 1) * size] = kept

    def remote(src, dst, send, recv, device):
        return pltpu.make_async_remote_copy(
            src_ref=src, dst_ref=dst, send_sem=send, recv_sem=recv,
            device_id=device, device_id_type=MESH,
        )

    def row_copy(zz, xx, n, send, device):
        ref = rowb.at[zz, rows_at(xx, n)]
        return remote(ref, ref, send, r_row.at[zz, xx, n], device)

    def up(zz, n):
        return row_copy(zz, x, n, s_up.at[zz, n], dev_z(z + 1))

    def down(zz, n):
        return row_copy(zz, x, n, s_dn.at[zz, n], dev_z(z - 1))

    def double(zz, n):
        return row_copy(zz, 1 - x, n, s_dup.at[jnp.where(zz == z, 0, 1), n], dev_z(inward))

    def across(zz, n):
        return row_copy(zz, x, n, s_x.at[zz, n], dev_x)

    def sideways(p, d, h):
        if p == 0:
            src = gb.at[0, gb_half(c, h)]
        else:
            src = rowb.at[ze, pl.ds(pl.multiple_of(x * length + h * side, side), side)]
        return remote(
            src, gb.at[p, gb_half(c, h)], s_y.at[p, d, h], r_gb.at[p, c, h], dev_y(d)
        )

    def to_twin(p, d):
        cc = lax.rem(y + d, yn) * 2 + k
        if p == 1 and d == 0:
            src = rowb.at[ze, pl.ds(x0, length)]
        else:
            src = gb.at[p, gb_panel(cc)]
        return remote(src, gb.at[p, gb_panel(cc)], s_c.at[p, d], r_tw.at[p, cc], dev_k)

    def got_row(zz, xx, n):
        row_copy(zz, xx, n, s_dup.at[0, n], dev_x).wait_recv()

    def got_side(p, d, h):
        cc = lax.rem(y + d, yn) * 2 + k
        ref = gb.at[p, gb_half(cc, h)]
        remote(ref, ref, s_dup.at[0, 0], r_gb.at[p, cc, h], dev_x).wait_recv()

    def got_twin(p, d):
        cc = lax.rem(y + d, yn) * 2 + 1 - k
        ref = gb.at[p, gb_panel(cc)]
        remote(ref, ref, s_dup.at[0, 0], r_tw.at[p, cc], dev_x).wait_recv()

    def own_sideways(h, do):
        for d in range(1, yn):
            do(sideways(0, d, h))

    def own_sends(n, do):
        if n < HALF:
            do(across(z, n))
        else:
            when(jnp.logical_not(proxy), lambda: do(across(z, n)))
        when(z < zn - 1, lambda: do(up(z, n)))
        when(z > 0, lambda: do(down(z, n)))
        if n == CHUNKS - 1:
            do(to_twin(0, 0))

    def y_arrivals(p, do, wait):
        for d in range(1, yn):
            if wait:
                for h in range(2):
                    got_side(p, d, h)
            do(to_twin(p, d))

    def relay(zz, n, do):
        @pl.when((zz < z) & (z + 1 <= zn - 2))
        def _():
            do(up(zz, n))

        @pl.when((zz > z) & (z - 1 >= 1))
        def _():
            do(down(zz, n))

        dist = jnp.abs(zz - z)
        twice = ((zz == 0) | (zz == zn - 1)) & (
            (dist == 1) | ((dist == 2) & (n >= LAST))
        )

        @pl.when(jnp.logical_not(twice))
        def _():
            do(across(zz, n))

        adjacent = proxy & (zz == ze)

        @pl.when(adjacent)
        def _():
            if n % HALF == HALF - 1:
                for d in range(1, yn):
                    do(sideways(1, d, n // HALF))
            if n == CHUNKS - 1:
                do(to_twin(1, 0))

    def inside(zz):
        return (zz >= 0) & (zz <= zn - 1)

    def start(copy):
        copy.start()

    def finish(copy):
        copy.wait_send()

    step_rows = 2 * length

    def product(p, block, panel, store):
        at = pl.ds(pl.multiple_of(block * step_rows, step_rows), step_rows)
        store(at, lax.dot_general(
            gb[p, at, :], panel[...], (((1,), (1,)), ((), ())),
            preferred_element_type=jnp.float32,
        ).astype(ob.dtype))

    def slot_of(gg, q):
        return lax.rem(gg + half_span - q + rows_n, rows_n)

    def own_job(zz):
        slots = [slot_of(g, row_of(zz, xx)) for xx in range(2)]

        def store(at, value):
            for xx in range(2):
                ob[slots[xx], at, :] = value[:, xx * length:(xx + 1) * length]

        def body(i, carry):
            product(0, i, rowb.at[zz], store)
            return carry

        lax.fori_loop(0, yn, body, 0)

    def proxy_copy(q, block):
        s = slot_of(row_of(ze, x), q)
        at = pl.ds(pl.multiple_of(block * step_rows, step_rows), step_rows)
        return remote(
            pb.at[q, at], ob.at[s, at], s_p.at[q, block], r_ob.at[s, block], dev_z(ze)
        )

    def proxy_job(zz, xx, low_d, high_d):
        q = row_of(zz, xx)

        def store(at, value):
            pb[q, at, :] = value

        def body(d, carry):
            block = lax.rem(y + d, yn)
            panel = rowb.at[zz, pl.ds(pl.multiple_of(xx * length, length), length)]
            product(1, block, panel, store)
            proxy_copy(q, block).start()
            return carry

        lax.fori_loop(low_d, high_d, body, 0)

    neighbours = 2 + (yn - 1)
    pl.semaphore_wait(barrier, neighbours + jnp.where(edge, 1, 2))

    for n in range(CHUNKS):
        own_sends(n, start)

        if n == HALF - 1:
            own_sideways(0, start)
        if n == CHUNKS - 1:
            when(edge, lambda: own_sideways(1, start))

    @pl.when(edge)
    def _():
        for n in range(CHUNKS):
            got_row(z, 1 - x, n)
            double(z, n).start()
            got_row(inward, x, n)
            across(inward, n).start()
        y_arrivals(0, start, True)
        for d in range(yn):
            got_twin(0, d)

        def job(j, carry):
            @pl.when(j == 1)
            def _():
                for n in range(CHUNKS):
                    got_row(inward, 1 - x, n)
                    if n >= HALF:
                        double(inward, n).start()

            own_job(jnp.where(j == 0, z, inward))
            return carry

        lax.fori_loop(0, 2, job, 0)

        for n in range(CHUNKS):
            own_sends(n, finish)
            double(z, n).wait_send()
            across(inward, n).wait_send()
            if n >= HALF:
                double(inward, n).wait_send()
        own_sideways(0, finish)
        own_sideways(1, finish)
        y_arrivals(0, finish, False)

        def far(i, carry):
            zz = inward + away * (i // 2 + 1)
            xx = jnp.where(lax.rem(i, 2) == 0, x, 1 - x)
            s = slot_of(g, row_of(zz, xx))
            for d in range(yn):
                block = lax.rem(y + d, yn)
                at = pl.ds(pl.multiple_of(block * step_rows, step_rows), step_rows)
                ref = ob.at[s, at]
                remote(ref, ref, s_p.at[0, 0], r_ob.at[s, block], dev_x).wait_recv()
            return carry

        lax.fori_loop(0, 2 * (zn - 2), far, 0)

    @pl.when(inner)
    def _():
        def settle():
            for n in range(CHUNKS):
                own_sends(n, finish)
            own_sideways(0, finish)
            own_sideways(1, finish)
            y_arrivals(0, finish, False)

            @pl.when(proxy)
            def _():
                y_arrivals(1, finish, False)
                for n in range(LAST, CHUNKS):
                    double(ze, n).wait_send()

            def relayed(zz, carry):
                @pl.when(zz != z)
                def _():
                    for n in range(CHUNKS):
                        relay(zz, n, finish)

                return carry

            lax.fori_loop(0, zn, relayed, 0)

        def turn(t, carry):
            first, second = t == 1, t == 2

            @pl.when(t == zn - 1)
            def _():
                settle()


            def forwards(n):
                for zz in (z - t * away, z + t * away):
                    @pl.when(inside(zz))
                    def _():
                        got_row(zz, x, n)
                        relay(zz, n, start)

                @pl.when(second & proxy)
                def _():
                    got_row(ze, 1 - x, n)
                    if n >= LAST:
                        double(ze, n).start()

            def proxied(dist, xx, low_d=0, high_d=yn):
                @pl.when(proxy & (dist >= 1) & inside(z + dist * away))
                def _():
                    proxy_job(z + dist * away, xx, low_d, high_d)

            def got_other(zz):
                @pl.when(inside(zz) & jnp.logical_not(proxy & (zz == ze)))
                def _():
                    for n in range(CHUNKS):
                        got_row(zz, 1 - x, n)

            for n in range(HALF):
                forwards(n)

            @pl.when(second & proxy)
            def _():
                y_arrivals(1, start, True)
                for d in range(1, yn):
                    got_twin(1, d)
                proxied(t - 1, x, 1)

            for n in range(HALF, CHUNKS):
                if n == CHUNKS - 1:
                    @pl.when(t > 1)
                    def _():
                        got_other(z + (t - 1) * away)
                        proxied(t - 1, 1 - x)
                forwards(n)

            @pl.when(first)
            def _():
                own_sideways(1, start)

            @pl.when(first & proxy)
            def _():
                gb[1, pl.ds(c0, length), :] = rowb[ze, pl.ds(x0, length), :]
                got_twin(1, 0)
                proxied(t, x, 0, 1)

            @pl.when(t > 1)
            def _():
                proxied(t, x)
                got_other(z - (t - 1) * away)

            @pl.when(second)
            def _():
                y_arrivals(0, start, True)
                for d in range(yn):
                    got_twin(0, d)

            def own(j, inner_carry):
                zz = z + jnp.where(j == 0, 1 - t, jnp.where(j == 1, t - 1, 0)) * away
                last = j == 2

                @pl.when(last & (t == zn - 1))
                def _():
                    for n in range(CHUNKS):
                        got_row(z, 1 - x, n)

                @pl.when(inside(zz) & (jnp.logical_not(last) | (t == zn - 1)))
                def _():
                    own_job(zz)

                return inner_carry

            @pl.when(t > 1)
            def _():
                lax.fori_loop(0, 3, own, 0)

            return carry

        lax.fori_loop(1, zn, turn, 0)

        @pl.when(proxy)
        def _():
            def sent(i, carry):
                zz = z + away * (i // 2 + 1)
                for d in range(yn):
                    proxy_copy(row_of(zz, lax.rem(i, 2)), d).wait_send()
                return carry

            lax.fori_loop(0, 2 * (zn - 2), sent, 0)


def local(density, pattern):
    rows_n, cols_n = lax.axis_size("row"), lax.axis_size("col")
    length, width = density.shape
    group = cols_n * length
    zn, yn = rows_n // 2, cols_n // 2
    kind = density.dtype
    dma = pltpu.SemaphoreType.DMA
    words = (2 * rows_n * group * length + (2 * group + rows_n * length + 2 * length) * width)
    out = pl.pallas_call(
        functools.partial(kernel, rows_n, cols_n),
        out_shape=jax.ShapeDtypeStruct((rows_n, group, length), kind),
        in_specs=[pl.BlockSpec(memory_space=pltpu.HBM)] * 2,
        out_specs=pl.BlockSpec(memory_space=pltpu.VMEM),
        scratch_shapes=[
            pltpu.VMEM((length, width), kind),
            pltpu.VMEM(pattern.shape, pattern.dtype),
            pltpu.VMEM((zn, 2 * length, width), kind),
            pltpu.VMEM((2, group, width), kind),
            pltpu.VMEM((rows_n, group, length), kind),
            dma((2,)),
            dma((zn, 2, CHUNKS)),
            dma((2, cols_n, 2)),
            dma((2, cols_n)),
            dma((rows_n, yn)),
            dma((zn, CHUNKS)),
            dma((zn, CHUNKS)),
            dma((2, CHUNKS)),
            dma((zn, CHUNKS)),
            dma((2, yn, 2)),
            dma((2, yn)),
            dma((rows_n, yn)),
        ],
        compiler_params=pltpu.CompilerParams(
            collective_id=0, has_side_effects=True, vmem_limit_bytes=2 * words + (8 << 20)
        ),
        cost_estimate=pl.CostEstimate(
            flops=2 * group * length * width * rows_n,
            bytes_accessed=2 * rows_n * group * length,
            transcendentals=0,
        ),
    )(*(pltpu.with_memory_space_constraint(a, pltpu.HBM) for a in (density, pattern)))
    return jnp.transpose(out, (1, 0, 2))


def solution(mesh):
    return jax.shard_map(
        local,
        mesh=mesh,
        in_specs=(P(("row", "col"), None), P(("row", "col"), None)),
        out_specs=P("row", None, "col"),
        check_vma=False,
    )
```
